512 devices in a mesh: dp: 128 (over x, z, y_hi, core), head: 4 (over y_lo).
Axes of the slice: x: 4, y: 8 (y_hi: 2, y_lo: 4; y = y_hi * 4 + y_lo), z: 8, core: 2. Of those that a mesh axis runs over, the one named last changes fastest.
Arguments:
- attn_queries: bfloat16 [65536, 1536], P('dp', 'head'), may hold values from -64 to 64
- keys: bfloat16 [65536, 256], P('dp'), may hold values from -6 to 6
- values: bfloat16 [65536, 256], P('dp'), may hold values from -6 to 6
- out_weight: bfloat16 [1536, 1536], P('head'), may hold values from -0.15625 to 0.15625
- lengths: int32 [128, 8], P('dp'), may hold values from 1 to 256, 512 in all within a row
- queries: bfloat16 [512, 1536], P('dp', 'head'), may hold values from -48 to 48
- positives: int32 [512], replicated, may hold values from 0 to 1023
Outputs:
- d_values: bfloat16 [65536, 256], P('dp', 'head')
- loss: float32 [], replicated
The draws below stay inside these ranges and needn't reach their ends.
Inputs may be any that keep to these rules, and one draw needn't show every extreme that they name: `lengths`: each row sums to 512.
All inputs are finite; a program needn't handle non-finite values.
Results may differ from the reference program's by a relative error of at most 0.0072.
Values may be sent and summed in bfloat16 or wider, within the bound.
No kernel may reach another device: no remote copies, remote signals or barrier semaphores. Data moves between devices by JAX's collectives and lax.ppermute only.
A program may use at most 64 MiB of HBM per device.

```python
import math
import jax
import jax.numpy as jnp
import numpy as np
from jax import lax

D = 1536
HEADS = 12
KV_HEADS = 2
HD = 128
TOK_DEV = 512
DOCS_DEV = 8
NDOC = 1024
NQ = 512
TOKENS = 65536
N_DP = 128


def draw_attn_queries(key, part):
    base_key = jax.random.fold_in(key, 11)
    normal = jnp.clip(jax.random.normal(base_key, (TOKENS, HEADS * HD), jnp.float32), -4.0, 4.0)
    return normal.astype(jnp.bfloat16)


def draw_queries(key, part):
    base_key = jax.random.fold_in(key, 21)
    normal = jnp.clip(jax.random.normal(base_key, (NQ, D), jnp.float32), -4.0, 4.0) / jnp.sqrt(1.0 * D)
    return normal.astype(jnp.bfloat16)


def with_ends(values, key, least, top_value):
    longest = values.shape.index(max(values.shape))
    spots = []
    for shift in (0, 1):
        where = [jax.random.randint(jax.random.fold_in(key, axis), (), 0, length) for axis, length in enumerate(values.shape)]
        where[longest] = (where[longest] + shift) % values.shape[longest]
        spots.append(tuple(where))
    return values.at[spots[0]].set(least).at[spots[1]].set(top_value)


def steps_of(key, extent, shards, smallest, high):
    factor_of = 1.0
    for position, parts in shards:
        steps = jax.random.uniform(jax.random.fold_in(jax.random.fold_in(key, 6), position), (parts,), jnp.float32, smallest / len(shards), high / len(shards))
        factor_of = factor_of * jnp.repeat(jnp.exp(steps), extent[position] // parts).reshape((-1,) + (1,) * (len(extent) - 1 - position))
    return factor_of


def profile(count, total, bound, skew):
    loads = [(1 << 20) // math.isqrt(grade ** skew) + 1 for grade in range(2, count + 1)]
    spare, holding = total - bound - (count - 1), [1] * (count - 1)
    while spare > 0:
        free = [i for i in range(count - 1) if holding[i] < bound]
        mass, left = sum([loads[i] for i in free]), spare
        for i in free:
            extra = min(bound - holding[i], max(1, left * loads[i] // mass), spare)
            holding[i] = holding[i] + extra
            spare = spare - extra
    return np.array([bound] + holding)


def uneven(stream_key, amount, total, most, lean):
    if amount == 2:
        one = jax.random.randint(stream_key, (), max(1, total - most), min(most, total - 1) + 1)
        return jnp.stack([one, total - one])
    sizes = jnp.asarray(profile(amount, total, most, lean), jnp.int32)
    couples = (amount - 1) // 2
    giver, taker = sizes[1:1 + 2 * couples:2], sizes[2:2 + 2 * couples:2]
    slack = jnp.minimum(giver - 1, most - taker)
    shifted = jax.random.randint(jax.random.fold_in(stream_key, 1), (couples,), 0, 1 << 20) % (slack + 1)
    sizes = sizes.at[1:1 + 2 * couples:2].set(giver - shifted).at[2:2 + 2 * couples:2].set(taker + shifted)
    return sizes[jax.random.permutation(jax.random.fold_in(stream_key, 2), amount)]


def normal_values(own_key, extent, deviation, most, pieces=(), held_as=jnp.bfloat16):
    values = jax.random.normal(own_key, extent, jnp.float32) * deviation
    if len(pieces) > 0:
        values = steps_of(own_key, extent, pieces, -0.22, 0.18) * values
    return jnp.clip(values, min=-most, max=most).astype(held_as)


def setup_inputs(seed: int = 0) -> dict:
    streams_of = jax.random.split(jax.random.key(seed), 8)
    attn_queries = draw_attn_queries(jax.random.fold_in(streams_of[7], 71), 0)
    keys = normal_values(streams_of[1], (TOKENS, KV_HEADS * HD), 1.0, 6.0, ((0, 128),))
    values = normal_values(streams_of[2], (TOKENS, KV_HEADS * HD), 1.0, 6.0, ((0, 128),))
    out_weight = normal_values(streams_of[3], (HEADS * HD, D), (HEADS * HD) ** -0.5, 0.15625, ((0, 4),))
    lengths = jax.vmap(lambda own: uneven(own, DOCS_DEV, TOK_DEV, TOK_DEV // 2, 2))(jax.random.split(streams_of[4], N_DP)).reshape((N_DP, DOCS_DEV)).astype(jnp.int32)
    queries = draw_queries(jax.random.fold_in(streams_of[7], 71), 0)
    positives = with_ends(jax.random.randint(streams_of[6], (NQ,), 0, NDOC), jax.random.fold_in(streams_of[6], 1), 0, NDOC - 1).astype(jnp.int32)
    return dict(attn_queries=attn_queries, keys=keys, values=values, out_weight=out_weight, lengths=lengths, queries=queries, positives=positives)


sim_scale = 20.0
loss_scale = 32768.0

def segment_ids(lens):
    ends = jnp.cumsum(lens)
    places = jnp.arange(TOK_DEV, dtype=jnp.int32)
    return lax.optimization_barrier(jnp.sum((places[:, None] >= ends[None, :]).astype(jnp.int32), axis=1))

def attend_probs(queries_h, keys_h, seg):
    scores = jnp.einsum('hqd,hkd->hqk', queries_h, keys_h, precision=lax.Precision.HIGHEST) / math.sqrt(HD)
    places = jnp.arange(TOK_DEV, dtype=jnp.int32)
    allowed = (seg[:, None] == seg[None, :]) & (places[None, :] <= places[:, None])
    scores = jnp.where(allowed[None], scores, -1e+30)
    top = lax.optimization_barrier(jnp.max(scores, axis=-1, keepdims=True))
    expo = jnp.exp(scores - top)
    return (expo / lax.optimization_barrier(jnp.sum(expo, axis=-1, keepdims=True))).astype(jnp.bfloat16)

def reference(attn_queries, keys, values, out_weight, lengths, queries, positives):
    width = HEADS * HD
    group = HEADS // KV_HEADS
    owner = jnp.arange(HEADS, dtype=jnp.int32) // group

    def split(array, index, count):
        piece = lax.dynamic_slice_in_dim(array, index * TOK_DEV, TOK_DEV, 0)
        return piece.reshape(TOK_DEV, count, HD).transpose(1, 0, 2).astype(jnp.float32)

    def member_of(seg):
        return jnp.arange(DOCS_DEV, dtype=jnp.int32)[:, None] == seg[None, :]

    def probs_of(index, seg):
        keys_all = split(keys, index, KV_HEADS)[owner]
        return attend_probs(split(attn_queries, index, HEADS), keys_all, seg)

    def forward(index):
        seg = segment_ids(lengths[index])
        probs = probs_of(index, seg)
        values_all = split(values, index, KV_HEADS)[owner]
        context = jnp.einsum('hqk,hkd->hqd', probs.astype(jnp.float32), values_all, precision=lax.Precision.HIGHEST)
        context = context.astype(jnp.bfloat16).transpose(1, 0, 2).reshape(TOK_DEV, width)
        sums = jnp.dot(member_of(seg).astype(jnp.bfloat16), context, preferred_element_type=jnp.float32)
        return sums / lengths[index][:, None].astype(jnp.float32)
    seq_index = jnp.arange(N_DP, dtype=jnp.int32)
    pooled = lax.map(forward, seq_index).reshape(N_DP * DOCS_DEV, width)
    weight = out_weight.astype(jnp.float32)
    emb = jnp.dot(pooled, weight, precision=lax.Precision.HIGHEST)
    rnorm = 1.0 / jnp.sqrt(lax.optimization_barrier(jnp.sum(emb * emb, axis=1)) + 1e-06)
    unit = emb * rnorm[:, None]
    unit_b = unit.astype(jnp.bfloat16)
    logits = sim_scale * jnp.dot(queries, unit_b.T, preferred_element_type=jnp.float32)
    top = lax.optimization_barrier(jnp.max(logits, axis=1))
    lse = top + jnp.log(lax.optimization_barrier(jnp.sum(jnp.exp(logits - top[:, None]), axis=1)))
    chosen = (jnp.arange(N_DP * DOCS_DEV, dtype=jnp.int32)[None, :] == positives[:, None]).astype(jnp.float32)
    pos_logit = lax.optimization_barrier(jnp.sum(logits * chosen, axis=1))
    loss = jnp.mean(lse - pos_logit)
    dlogits = jnp.exp(logits - lse[:, None]) - chosen
    g_unit = sim_scale * jnp.dot(dlogits.T, queries.astype(jnp.float32), precision=lax.Precision.HIGHEST)
    inner = lax.optimization_barrier(jnp.sum(unit * g_unit, axis=1))
    g_emb = rnorm[:, None] * (g_unit - unit * inner[:, None])
    g_pooled = jnp.dot(g_emb, weight.T, precision=lax.Precision.HIGHEST)

    def backward(index):
        seg = segment_ids(lengths[index])
        probs = probs_of(index, seg)
        rows = lax.dynamic_slice_in_dim(g_pooled, index * DOCS_DEV, DOCS_DEV, 0)
        scaled = rows / lengths[index][:, None].astype(jnp.float32) * loss_scale
        d_context = jnp.dot(member_of(seg).astype(jnp.float32).T, scaled, precision=lax.Precision.HIGHEST)
        d_context = d_context.astype(jnp.bfloat16).reshape(TOK_DEV, HEADS, HD).transpose(1, 0, 2).astype(jnp.float32)
        grads = jnp.einsum('hqk,hqd->hkd', probs.astype(jnp.float32), d_context, precision=lax.Precision.HIGHEST)
        grads = lax.optimization_barrier(jnp.sum(grads.reshape(KV_HEADS, group, TOK_DEV, HD), axis=1))
        return grads.astype(jnp.bfloat16).transpose(1, 0, 2).reshape(TOK_DEV, KV_HEADS * HD)
    d_values = lax.map(backward, seq_index).reshape(N_DP * TOK_DEV, KV_HEADS * HD)
    return (d_values, loss)
```

```python
import math

import jax
import jax.numpy as jnp
from jax import lax
from jax.experimental import pallas as pl
from jax.experimental.pallas import tpu as pltpu
from jax.sharding import Mesh
from jax.sharding import PartitionSpec as P

HEADS = 12
KV_HEADS = 2
HD = 128
DP = ("dp_0", "dp_1", "dp_2", "dp_3")
LONGEST = 256

sim_scale = 20.0
loss_scale = 32768.0

NT = (((1,), (1,)), ((), ()))
TN = (((0,), (0,)), ((), ()))
VMEM = pl.BlockSpec(memory_space=pltpu.VMEM)
SMEM = pl.BlockSpec(memory_space=pltpu.SMEM)


def three_terms(value):
    high = value.astype(jnp.bfloat16)
    rest = value - high.astype(jnp.float32)
    mid = rest.astype(jnp.bfloat16)
    low = (rest - mid.astype(jnp.float32)).astype(jnp.bfloat16)
    return jnp.concatenate([high, mid, low], axis=0)


def of_three(value):
    rows = value.shape[0] // 3
    return value[:rows] + value[rows : 2 * rows] + value[2 * rows :]


def exact_dot(value, other, dims):
    return of_three(
        lax.dot_general(three_terms(value), other, dims, preferred_element_type=jnp.float32)
    )


def document_of(lens_ref, docs, shape, dim):
    place = lax.broadcasted_iota(jnp.int32, shape, dim)
    seg = jnp.zeros(shape, jnp.int32)
    start = jnp.zeros(shape, jnp.int32)
    end = jnp.int32(0)
    for j in range(docs):
        end = end + lens_ref[0, j]
        past = place >= end
        seg = seg + past.astype(jnp.int32)
        start = jnp.where(past, end, start)
    return seg, start


def lens_column(lens_ref, docs):
    row = lax.broadcasted_iota(jnp.int32, (docs, 1), 0)
    column = jnp.zeros((docs, 1), jnp.int32)
    for j in range(docs):
        column = jnp.where(row == j, lens_ref[0, j], column)
    return column.astype(jnp.float32)


def attend_kernel(lens_ref, q_ref, k_ref, v_ref, w_ref, out_ref, total):
    seq_len, width = q_ref.shape
    heads = width // HD
    docs = lens_ref.shape[1]
    features = w_ref.shape[1]
    kv_head = lax.axis_index("head") * heads // (HEADS // KV_HEADS)
    columns = pl.ds(pl.multiple_of(kv_head * HD, HD), HD)
    seg, start = document_of(lens_ref, docs, (1, seq_len), 1)
    total[...] = jnp.zeros_like(total)
    block = min(128, seq_len)
    factor = math.log2(math.e) / math.sqrt(HD)
    lane = lax.broadcasted_iota(jnp.int32, (block, HD), 1)
    for first in range(0, seq_len, block):
        low = max(0, (first - LONGEST + 1) // block * block)
        span = first + block - low
        k_block = k_ref[low : first + block, columns]
        k_place = low + lax.broadcasted_iota(jnp.int32, (span, block), 0)
        q_place = first + lax.broadcasted_iota(jnp.int32, (span, block), 1)
        allowed = (k_place <= q_place) & (k_place >= start[:, first : first + block])
        for h in range(heads):
            q_block = q_ref[first : first + block, h * HD : (h + 1) * HD]
            scores = lax.dot_general(k_block, q_block, NT, preferred_element_type=jnp.float32)
            scores = jnp.where(allowed, scores, -1e30)
            top = jnp.max(scores, axis=0, keepdims=True)
            expo = jnp.exp2((scores - top) * factor)
            norm = 1.0 / jnp.sum(expo, axis=0, keepdims=True)
            probs = (expo * norm).astype(jnp.bfloat16)
            pick = (lane == h).astype(jnp.bfloat16)
            total[low : first + block, :] += jnp.dot(
                probs, pick, preferred_element_type=jnp.float32
            )
    by_head = total[...].T
    member = lax.broadcasted_iota(jnp.int32, (docs, seq_len), 0) == seg
    shares = jnp.concatenate(
        [jnp.where(member, by_head[h : h + 1, :], 0.0) for h in range(heads)], axis=0
    )
    sums = exact_dot(shares, v_ref[:, columns], (((1,), (0,)), ((), ())))
    pooled = jnp.concatenate(
        [sums[h * docs : (h + 1) * docs] for h in range(heads)], axis=1
    ) / lens_column(lens_ref, docs)
    emb = exact_dot(pooled, w_ref[...], (((1,), (0,)), ((), ())))
    for k in range(out_ref.shape[0]):
        out_ref[k, :, :features] = emb
        out_ref[k, :, features:] = by_head[:docs, :]


def logits_kernel(emb_ref, q_ref, pos_ref, out_ref, logits_ref, unit_ref, rnorm_ref):
    docs = emb_ref.shape[1]
    features = q_ref.shape[1]
    emb = emb_ref[0, :, :features]
    for k in range(1, emb_ref.shape[0]):
        emb = emb + emb_ref[k, :, :features]
    rnorm = 1.0 / jnp.sqrt(jnp.sum(emb * emb, axis=1, keepdims=True) + 1e-06)
    unit = emb * rnorm
    logits = sim_scale * lax.dot_general(
        unit.astype(jnp.bfloat16), q_ref[...], NT, preferred_element_type=jnp.float32
    )
    chosen = positive_mask(pos_ref, docs)
    top = jnp.max(logits, axis=0, keepdims=True)
    lse = top + jnp.log(jnp.sum(jnp.exp(logits - top), axis=0, keepdims=True))
    positive = jnp.sum(jnp.where(chosen, logits, 0.0), axis=0, keepdims=True)
    out_ref[...] = jnp.broadcast_to(
        jnp.concatenate([lse, positive], axis=0)[None], out_ref.shape
    )
    logits_ref[...] = logits
    unit_ref[...] = unit
    rnorm_ref[...] = jnp.broadcast_to(rnorm, rnorm_ref.shape)


def positive_mask(pos_ref, docs):
    count = pos_ref.shape[1]
    positive = pos_ref[pl.ds(lax.axis_index("head"), 1), :]
    owned = lax.axis_index(DP) * docs + lax.broadcasted_iota(jnp.int32, (docs, count), 0)
    return positive == owned


def slopes_kernel(stats_ref, logits_ref, q_ref, pos_ref, out_ref):
    docs = logits_ref.shape[0]
    features = q_ref.shape[1]
    each = stats_ref[:, 0, :]
    top = jnp.max(each, axis=0, keepdims=True)
    lse = top + jnp.log(jnp.sum(jnp.exp(each - top), axis=0, keepdims=True))
    positive = jnp.sum(stats_ref[:, 1, :], axis=0, keepdims=True)
    chosen = positive_mask(pos_ref, docs)
    slopes = jnp.exp(logits_ref[...] - lse) - chosen.astype(jnp.float32)
    grads = sim_scale * exact_dot(slopes, q_ref[...], (((1,), (0,)), ((), ())))
    losses = jnp.broadcast_to(lse - positive, (docs, lse.shape[1]))
    for k in range(out_ref.shape[0]):
        out_ref[k, :, :features] = grads
        out_ref[k, :, features:] = losses


def context_kernel(lens_ref, grads_ref, unit_ref, rnorm_ref, w_ref, kept_ref, sent_ref, loss_ref):
    docs, features = unit_ref.shape
    heads = w_ref.shape[0] // HD
    half = HD // 2
    grads = grads_ref[0]
    for k in range(1, grads_ref.shape[0]):
        grads = grads + grads_ref[k]
    count = grads_ref.shape[0] * (grads.shape[1] - features)
    loss_ref[...] = jnp.sum(grads[:1, features:], axis=1, keepdims=True) / count
    grads = grads[:, :features]
    unit = unit_ref[...]
    inner = jnp.sum(unit * grads, axis=1, keepdims=True)
    g_emb = rnorm_ref[:, :1] * (grads - unit * inner)
    g_pooled = exact_dot(g_emb, w_ref[...], NT)
    scaled = (g_pooled / lens_column(lens_ref, docs) * loss_scale).astype(jnp.bfloat16)
    rows = jnp.concatenate(
        [scaled[:, h * HD : (h + 1) * HD] for h in range(heads)], axis=0
    )
    odd = lax.axis_index("head") % 2 == 1
    lower, upper = rows[:, :half], rows[:, half:]
    kept_ref[...] = jnp.where(odd, upper, lower)
    sent_ref[...] = jnp.where(odd, lower, upper)


def values_kernel(lens_ref, emb_ref, mine_ref, theirs_ref, out_ref):
    docs = emb_ref.shape[1]
    seq_len = out_ref.shape[0]
    heads = mine_ref.shape[0] // docs
    me = lax.axis_index("head")
    partner = me + 1 - 2 * (me % 2)
    seg, _ = document_of(lens_ref, docs, (1, seq_len), 1)
    member = lax.broadcasted_iota(jnp.int32, (docs, seq_len), 0) == seg
    features = emb_ref.shape[2] - seq_len
    shares = []
    for owner in (me, partner):
        by_head = emb_ref[owner, :, features:]
        shares += [jnp.where(member, by_head[h : h + 1, :], 0.0) for h in range(heads)]
    slopes = jnp.concatenate([mine_ref[...], theirs_ref[...]], axis=0)
    out = lax.dot_general(
        three_terms(jnp.concatenate(shares, axis=0)),
        jnp.concatenate([slopes] * 3, axis=0),
        TN,
        preferred_element_type=jnp.float32,
    )
    out_ref[...] = out.astype(jnp.bfloat16)


def per_device(attn_queries, keys, values, out_weight, lengths, queries, positives):
    seq_len, width = attn_queries.shape
    heads = width // HD
    docs = lengths.shape[1]
    features = out_weight.shape[1]
    split = lax.axis_size("head")
    cores = lax.axis_size(DP[3])
    others = lax.axis_size(DP[:3])
    n_dp = cores * others
    f32, bf16 = jnp.float32, jnp.bfloat16

    rows = jnp.broadcast_to(queries[None], (cores, *queries.shape)).reshape(cores * split, 1, -1)
    rows = lax.all_to_all(rows, (DP[3], "head"), 0, 0, tiled=True).reshape(cores, features)
    rows = jnp.broadcast_to(rows[None], (others, cores, features))
    every = lax.all_to_all(rows, DP[:3], 0, 0, tiled=True).reshape(n_dp, features)
    pos = positives.reshape(n_dp, split).T

    partial = pl.pallas_call(
        attend_kernel,
        out_shape=jax.ShapeDtypeStruct((split, docs, features + seq_len), f32),
        in_specs=[SMEM] + [VMEM] * 4,
        out_specs=VMEM,
        scratch_shapes=[pltpu.VMEM((seq_len, HD), f32)],
        compiler_params=pltpu.CompilerParams(vmem_limit_bytes=32 * 2**20),
        name="attend",
    )(lengths, attn_queries, keys, values, out_weight)
    partial = lax.all_to_all(partial, "head", 0, 0, tiled=True)

    stats, logits, unit, rnorm = pl.pallas_call(
        logits_kernel,
        out_shape=(
            jax.ShapeDtypeStruct((n_dp, 2, n_dp), f32),
            jax.ShapeDtypeStruct((docs, n_dp), f32),
            jax.ShapeDtypeStruct((docs, features), f32),
            jax.ShapeDtypeStruct((docs, HD), f32),
        ),
        in_specs=[VMEM] * 3,
        out_specs=(VMEM,) * 4,
        name="logits",
    )(partial, every, pos)
    stats = lax.all_to_all(stats, DP, 0, 0, tiled=True)

    grads = pl.pallas_call(
        slopes_kernel,
        out_shape=jax.ShapeDtypeStruct((split, docs, features + n_dp), f32),
        in_specs=[VMEM] * 4,
        out_specs=VMEM,
        name="slopes",
    )(stats, logits, every, pos)
    grads = lax.all_to_all(grads, "head", 0, 0, tiled=True)

    kept, sent, loss = pl.pallas_call(
        context_kernel,
        out_shape=(
            jax.ShapeDtypeStruct((heads * docs, HD // 2), bf16),
            jax.ShapeDtypeStruct((heads * docs, HD // 2), bf16),
            jax.ShapeDtypeStruct((1, 1), f32),
        ),
        in_specs=[SMEM] + [VMEM] * 4,
        out_specs=(VMEM,) * 3,
        name="context",
    )(lengths, grads, unit, rnorm, out_weight)
    got = lax.ppermute(sent, "head", [(i, i ^ 1) for i in range(split)])

    d_values = pl.pallas_call(
        values_kernel,
        out_shape=jax.ShapeDtypeStruct((seq_len, HD // 2), bf16),
        in_specs=[SMEM] + [VMEM] * 3,
        out_specs=VMEM,
        name="slopes_of_values",
    )(lengths, partial, kept, got)
    return d_values, loss.reshape(())


def solution(mesh):
    shape = (4, 8, 2, 2) if mesh.devices.size == 512 else (1, mesh.devices.size // 16, 2, 2)
    torus = Mesh(mesh.devices.reshape(*shape, mesh.shape["head"]), (*DP, "head"))
    placed = (
        P(DP, "head"),
        P(DP, None),
        P(DP, None),
        P("head", None),
        P(DP, None),
        P(DP, "head"),
        P(),
    )
    return jax.shard_map(
        per_device, mesh=torus, in_specs=placed, out_specs=(P(DP, "head"), P()), check_vma=False
    )
```

```python
import math

import jax
import jax.numpy as jnp
from jax import lax
from jax.experimental import pallas as pl
from jax.experimental.pallas import tpu as pltpu
from jax.sharding import Mesh
from jax.sharding import PartitionSpec as P

HEADS = 12
KV_HEADS = 2
HD = 128
DP = ("dp_0", "dp_1", "dp_2", "dp_3")
LONGEST = 256

sim_scale = 20.0
loss_scale = 32768.0

NT = (((1,), (1,)), ((), ()))
TN = (((0,), (0,)), ((), ()))
VMEM = pl.BlockSpec(memory_space=pltpu.VMEM)
SMEM = pl.BlockSpec(memory_space=pltpu.SMEM)


def three_terms(value):
    high = value.astype(jnp.bfloat16)
    rest = value - high.astype(jnp.float32)
    mid = rest.astype(jnp.bfloat16)
    low = (rest - mid.astype(jnp.float32)).astype(jnp.bfloat16)
    return jnp.concatenate([high, mid, low], axis=0)


def of_three(value):
    rows = value.shape[0] // 3
    return value[:rows] + value[rows : 2 * rows] + value[2 * rows :]


def exact_dot(value, other, dims):
    return of_three(
        lax.dot_general(three_terms(value), other, dims, preferred_element_type=jnp.float32)
    )


def document_of(lens_ref, docs, shape, dim):
    place = lax.broadcasted_iota(jnp.int32, shape, dim)
    seg = jnp.zeros(shape, jnp.int32)
    start = jnp.zeros(shape, jnp.int32)
    end = jnp.int32(0)
    for j in range(docs):
        end = end + lens_ref[0, j]
        past = place >= end
        seg = seg + past.astype(jnp.int32)
        start = jnp.where(past, end, start)
    return seg, start


def lens_column(lens_ref, docs):
    row = lax.broadcasted_iota(jnp.int32, (docs, 1), 0)
    column = jnp.zeros((docs, 1), jnp.int32)
    for j in range(docs):
        column = jnp.where(row == j, lens_ref[0, j], column)
    return column.astype(jnp.float32)


def attend_kernel(lens_ref, q_ref, k_ref, v_ref, w_ref, out_ref, sums_ref, total):
    seq_len, width = q_ref.shape
    heads = width // HD
    docs = lens_ref.shape[1]
    kv_head = lax.axis_index("head") * heads // (HEADS // KV_HEADS)
    columns = pl.ds(pl.multiple_of(kv_head * HD, HD), HD)
    seg, start = document_of(lens_ref, docs, (1, seq_len), 1)
    total[...] = jnp.zeros_like(total)
    block = min(128, seq_len)
    factor = math.log2(math.e) / math.sqrt(HD)
    lane = lax.broadcasted_iota(jnp.int32, (block, HD), 1)
    for first in range(0, seq_len, block):
        low = max(0, (first - LONGEST + 1) // block * block)
        span = first + block - low
        k_block = k_ref[low : first + block, columns]
        k_place = low + lax.broadcasted_iota(jnp.int32, (span, block), 0)
        q_place = first + lax.broadcasted_iota(jnp.int32, (span, block), 1)
        allowed = (k_place <= q_place) & (k_place >= start[:, first : first + block])
        for h in range(heads):
            q_block = q_ref[first : first + block, h * HD : (h + 1) * HD]
            scores = lax.dot_general(k_block, q_block, NT, preferred_element_type=jnp.float32)
            scores = jnp.where(allowed, scores, -1e30)
            top = jnp.max(scores, axis=0, keepdims=True)
            expo = jnp.exp2((scores - top) * factor)
            norm = 1.0 / jnp.sum(expo, axis=0, keepdims=True)
            probs = (expo * norm).astype(jnp.bfloat16)
            pick = (lane == h).astype(jnp.bfloat16)
            total[low : first + block, :] += jnp.dot(
                probs, pick, preferred_element_type=jnp.float32
            )
    by_head = total[...].T
    member = lax.broadcasted_iota(jnp.int32, (docs, seq_len), 0) == seg
    shares = jnp.concatenate(
        [jnp.where(member, by_head[h : h + 1, :], 0.0) for h in range(heads)], axis=0
    )
    sums = exact_dot(shares, v_ref[:, columns], (((1,), (0,)), ((), ())))
    pooled = jnp.concatenate(
        [sums[h * docs : (h + 1) * docs] for h in range(heads)], axis=1
    ) / lens_column(lens_ref, docs)
    emb = exact_dot(pooled, w_ref[...], (((1,), (0,)), ((), ())))
    out_ref[...] = emb
    sums_ref[...] = by_head[:docs, :]


def pair_logits(unit, q_ref):
    half = q_ref.shape[1]
    docs = unit.shape[0]
    both = jnp.concatenate([unit[:, :half], unit[:, half:]], axis=0)
    parts = lax.dot_general(both, q_ref[...], NT, preferred_element_type=jnp.float32)
    even = lax.broadcasted_iota(jnp.int32, (docs, q_ref.shape[0]), 1) % 2 == 0
    mine = jnp.where(even, parts[:docs], parts[docs:])
    width = mine.shape[1]
    other = jnp.where(even, pltpu.roll(mine, width - 1, 1), pltpu.roll(mine, 1, 1))
    return sim_scale * (mine + other)


def positive_mask(pos_ref, docs):
    count = pos_ref.shape[1]
    positive = pos_ref[pl.ds(lax.axis_index((DP[3], "head")), 1), :]
    owned = lax.axis_index(DP[:3]) * docs + lax.broadcasted_iota(jnp.int32, (docs, count), 0)
    return positive == owned


def logits_kernel(emb_ref, q_ref, pos_ref, out_ref, logits_ref, unit_ref, rnorm_ref):
    emb = jnp.concatenate([emb_ref[k] for k in range(emb_ref.shape[0])], axis=0)
    rnorm = 1.0 / jnp.sqrt(jnp.sum(emb * emb, axis=1, keepdims=True) + 1e-06)
    unit = emb * rnorm
    logits = pair_logits(unit.astype(jnp.bfloat16), q_ref)
    chosen = positive_mask(pos_ref, emb.shape[0])
    top = jnp.max(logits, axis=0, keepdims=True)
    lse = top + jnp.log(jnp.sum(jnp.exp(logits - top), axis=0, keepdims=True))
    positive = jnp.sum(jnp.where(chosen, logits, 0.0), axis=0, keepdims=True)
    out_ref[...] = jnp.broadcast_to(
        jnp.concatenate([lse, positive], axis=0)[None], out_ref.shape
    )
    logits_ref[...] = logits
    unit_ref[...] = unit
    rnorm_ref[...] = jnp.broadcast_to(rnorm, rnorm_ref.shape)


def slopes_kernel(stats_ref, logits_ref, unit_ref, rnorm_ref, q_ref, pos_ref, out_ref):
    pair_docs = logits_ref.shape[0]
    half = q_ref.shape[1]
    features = 2 * half
    split = out_ref.shape[0] // 2
    docs = pair_docs // 2
    each = stats_ref[:, 0, :]
    top = jnp.max(each, axis=0, keepdims=True)
    lse = top + jnp.log(jnp.sum(jnp.exp(each - top), axis=0, keepdims=True))
    positive = jnp.sum(stats_ref[:, 1, :], axis=0, keepdims=True)
    chosen = positive_mask(pos_ref, pair_docs)
    slopes = jnp.exp(logits_ref[...] - lse) - chosen.astype(jnp.float32)
    even = lax.broadcasted_iota(jnp.int32, slopes.shape, 1) % 2 == 0
    both = jnp.concatenate([jnp.where(even, slopes, 0.0), jnp.where(even, 0.0, slopes)], axis=0)
    parts = sim_scale * exact_dot(both, q_ref[...], (((1,), (0,)), ((), ())))
    grads = jnp.concatenate([parts[:pair_docs], parts[pair_docs:]], axis=1)
    unit = unit_ref[...]
    inner = jnp.sum(unit * grads, axis=1, keepdims=True)
    grads = (rnorm_ref[:, :1] * (grads - unit * inner)).astype(jnp.bfloat16)
    losses = jnp.broadcast_to(lse - positive, (docs, lse.shape[1]))
    row = lax.broadcasted_iota(jnp.int32, losses.shape, 0)
    high = losses.astype(jnp.bfloat16).astype(jnp.float32)
    mid = (losses - high).astype(jnp.bfloat16).astype(jnp.float32)
    losses = jnp.where(row == 0, high, jnp.where(row == 1, mid, losses - high - mid))
    for k in range(2 * split):
        core = k // split
        out_ref[k, :, :features] = grads[core * docs : (core + 1) * docs]
        out_ref[k, :, features:] = losses.astype(jnp.bfloat16)


def context_kernel(lens_ref, grads_ref, w_ref, kept_ref, sent_ref, loss_ref):
    docs = lens_ref.shape[1]
    features = w_ref.shape[1]
    heads = w_ref.shape[0] // HD
    half = HD // 2
    grads = grads_ref[0].astype(jnp.float32)
    for k in range(1, grads_ref.shape[0]):
        grads = grads + grads_ref[k].astype(jnp.float32)
    lanes = grads.shape[1] - features
    count = grads_ref.shape[0] * lanes
    loss_ref[...] = (
        jnp.sum(jnp.sum(grads[:3, features:], axis=0, keepdims=True), axis=1, keepdims=True) / count
    )
    g_pooled = exact_dot(grads[:, :features], w_ref[...], NT)
    scaled = (g_pooled / lens_column(lens_ref, docs) * loss_scale).astype(jnp.bfloat16)
    rows = jnp.concatenate(
        [scaled[:, h * HD : (h + 1) * HD] for h in range(heads)], axis=0
    )
    odd = lax.axis_index("head") % 2 == 1
    lower, upper = rows[:, :half], rows[:, half:]
    kept_ref[...] = jnp.where(odd, upper, lower)
    sent_ref[...] = jnp.where(odd, lower, upper)


def values_kernel(lens_ref, my_sums_ref, their_sums_ref, mine_ref, theirs_ref, out_ref):
    docs = lens_ref.shape[1]
    seq_len = out_ref.shape[1]
    heads = mine_ref.shape[0] // docs
    seg, _ = document_of(lens_ref, docs, (1, seq_len), 1)
    member = lax.broadcasted_iota(jnp.int32, (docs, seq_len), 0) == seg
    shares = []
    for sums in (my_sums_ref, their_sums_ref):
        shares += [jnp.where(member, sums[h : h + 1, :], 0.0) for h in range(heads)]
    slopes = jnp.concatenate([mine_ref[...], theirs_ref[...]], axis=0)
    out = lax.dot_general(
        jnp.concatenate([slopes] * 3, axis=0),
        three_terms(jnp.concatenate(shares, axis=0)),
        TN,
        preferred_element_type=jnp.float32,
    )
    out_ref[...] = out.astype(jnp.bfloat16)


def per_device(attn_queries, keys, values, out_weight, lengths, queries, positives):
    seq_len, width = attn_queries.shape
    heads = width // HD
    docs = lengths.shape[1]
    features = out_weight.shape[1]
    split = lax.axis_size("head")
    cores = lax.axis_size(DP[3])
    others = lax.axis_size(DP[:3])
    lanes = 2 * others
    f32, bf16 = jnp.float32, jnp.bfloat16
    big = pltpu.CompilerParams(vmem_limit_bytes=60 * 2**20)

    row = lax.all_to_all(queries.reshape(split, 1, -1), "head", 0, 0, tiled=True)
    emb, sums = pl.pallas_call(
        attend_kernel,
        out_shape=(
            jax.ShapeDtypeStruct((docs, features), f32),
            jax.ShapeDtypeStruct((docs, seq_len), f32),
        ),
        in_specs=[SMEM] + [VMEM] * 4,
        out_specs=(VMEM, VMEM),
        scratch_shapes=[pltpu.VMEM((seq_len, HD), f32)],
        compiler_params=big,
        name="attend",
    )(lengths, attn_queries, keys, values, out_weight)
    row, emb, sums = lax.optimization_barrier((row, emb, sums))
    rows = jnp.broadcast_to(row.reshape(1, 2, features // 2), (others, 2, features // 2))
    every = lax.all_to_all(rows, DP[:3], 0, 0, tiled=True).reshape(lanes, features // 2)
    pos = jnp.repeat(positives.reshape(others, cores * split).T, 2, axis=1)

    whole = emb
    for apart in range(1, split):
        whole = whole + lax.ppermute(emb, "head", [(i, i ^ apart) for i in range(split)])
    their_sums = lax.ppermute(sums, "head", [(i, i ^ 1) for i in range(split)])
    pair = lax.all_gather(whole, DP[3])

    stats, logits, unit, rnorm = pl.pallas_call(
        logits_kernel,
        out_shape=(
            jax.ShapeDtypeStruct((others, 2, lanes), f32),
            jax.ShapeDtypeStruct((cores * docs, lanes), f32),
            jax.ShapeDtypeStruct((cores * docs, features), f32),
            jax.ShapeDtypeStruct((cores * docs, HD), f32),
        ),
        in_specs=[VMEM] * 3,
        out_specs=(VMEM,) * 4,
        name="logits",
    )(pair, every, pos)
    stats = lax.all_to_all(stats, DP[:3], 0, 0, tiled=True)

    grads = pl.pallas_call(
        slopes_kernel,
        out_shape=jax.ShapeDtypeStruct((cores * split, docs, features + lanes), bf16),
        in_specs=[VMEM] * 6,
        out_specs=VMEM,
        name="slopes",
    )(stats, logits, unit, rnorm, every, pos)
    grads = lax.all_to_all(grads, (DP[3], "head"), 0, 0, tiled=True)

    kept, sent, loss = pl.pallas_call(
        context_kernel,
        out_shape=(
            jax.ShapeDtypeStruct((heads * docs, HD // 2), bf16),
            jax.ShapeDtypeStruct((heads * docs, HD // 2), bf16),
            jax.ShapeDtypeStruct((1, 1), f32),
        ),
        in_specs=[SMEM] + [VMEM] * 2,
        out_specs=(VMEM,) * 3,
        name="context",
    )(lengths, grads, out_weight)
    got = lax.ppermute(sent, "head", [(i, i ^ 1) for i in range(split)])

    d_values = pl.pallas_call(
        values_kernel,
        out_shape=jax.ShapeDtypeStruct((HD // 2, seq_len), bf16),
        in_specs=[SMEM] + [VMEM] * 4,
        out_specs=VMEM,
        name="slopes_of_values",
    )(lengths, sums, their_sums, kept, got)
    return d_values.T, loss.reshape(())


def solution(mesh):
    shape = (4, 8, 2, 2) if mesh.devices.size == 512 else (1, mesh.devices.size // 16, 2, 2)
    torus = Mesh(mesh.devices.reshape(*shape, mesh.shape["head"]), (*DP, "head"))
    placed = (
        P(DP, "head"),
        P(DP, None),
        P(DP, None),
        P("head", None),
        P(DP, None),
        P(DP, "head"),
        P(),
    )
    return jax.shard_map(
        per_device, mesh=torus, in_specs=placed, out_specs=(P(DP, "head"), P()), check_vma=False
    )
```

```python
import math

import jax
import jax.numpy as jnp
from jax import lax
from jax.experimental import pallas as pl
from jax.experimental.pallas import tpu as pltpu
from jax.sharding import Mesh
from jax.sharding import PartitionSpec as P

HEADS = 12
KV_HEADS = 2
HD = 128
DP = ("dp_0", "dp_1", "dp_2", "dp_3")
LONGEST = 256
HEAD = ("head_0", "head_1")

sim_scale = 20.0
loss_scale = 32768.0

NT = (((1,), (1,)), ((), ()))
TN = (((0,), (0,)), ((), ()))
VMEM = pl.BlockSpec(memory_space=pltpu.VMEM)
SMEM = pl.BlockSpec(memory_space=pltpu.SMEM)


def three_terms(value):
    high = value.astype(jnp.bfloat16)
    rest = value - high.astype(jnp.float32)
    mid = rest.astype(jnp.bfloat16)
    low = (rest - mid.astype(jnp.float32)).astype(jnp.bfloat16)
    return jnp.concatenate([high, mid, low], axis=0)


def of_three(value):
    rows = value.shape[0] // 3
    return value[:rows] + value[rows : 2 * rows] + value[2 * rows :]


def exact_dot(value, other, dims):
    return of_three(
        lax.dot_general(three_terms(value), other, dims, preferred_element_type=jnp.float32)
    )


def document_of(lens_ref, docs, shape, dim):
    place = lax.broadcasted_iota(jnp.int32, shape, dim)
    seg = jnp.zeros(shape, jnp.int32)
    start = jnp.zeros(shape, jnp.int32)
    end = jnp.int32(0)
    for j in range(docs):
        end = end + lens_ref[0, j]
        past = place >= end
        seg = seg + past.astype(jnp.int32)
        start = jnp.where(past, end, start)
    return seg, start


def lens_column(lens_ref, docs):
    row = lax.broadcasted_iota(jnp.int32, (docs, 1), 0)
    column = jnp.zeros((docs, 1), jnp.int32)
    for j in range(docs):
        column = jnp.where(row == j, lens_ref[0, j], column)
    return column.astype(jnp.float32)


def attend_kernel(lens_ref, q_ref, k_ref, v_ref, w_ref, out_ref, total):
    seq_len, width = q_ref.shape
    heads = width // HD
    docs = lens_ref.shape[1]
    kv_head = lax.axis_index(HEAD) * heads // (HEADS // KV_HEADS)
    columns = pl.ds(pl.multiple_of(kv_head * HD, HD), HD)
    seg, start = document_of(lens_ref, docs, (1, seq_len), 1)
    total[...] = jnp.zeros_like(total)
    block = min(128, seq_len)
    factor = math.log2(math.e) / math.sqrt(HD)
    lane = lax.broadcasted_iota(jnp.int32, (block, HD), 1)
    for first in range(0, seq_len, block):
        low = max(0, (first - LONGEST + 1) // block * block)
        span = first + block - low
        k_block = k_ref[low : first + block, columns]
        k_place = low + lax.broadcasted_iota(jnp.int32, (span, block), 0)
        q_place = first + lax.broadcasted_iota(jnp.int32, (span, block), 1)
        allowed = (k_place <= q_place) & (k_place >= start[:, first : first + block])
        for h in range(heads):
            q_block = q_ref[first : first + block, h * HD : (h + 1) * HD]
            scores = lax.dot_general(k_block, q_block, NT, preferred_element_type=jnp.float32)
            scores = jnp.where(allowed, scores, -1e30)
            top = jnp.max(scores, axis=0, keepdims=True)
            expo = jnp.exp2((scores - top) * factor)
            norm = 1.0 / jnp.sum(expo, axis=0, keepdims=True)
            probs = (expo * norm).astype(jnp.bfloat16)
            pick = (lane == h).astype(jnp.bfloat16)
            total[low : first + block, :] += jnp.dot(
                probs, pick, preferred_element_type=jnp.float32
            )
    by_head = total[...].T
    member = lax.broadcasted_iota(jnp.int32, (docs, seq_len), 0) == seg
    shares = jnp.concatenate(
        [jnp.where(member, by_head[h : h + 1, :], 0.0) for h in range(heads)], axis=0
    )
    sums = exact_dot(shares, v_ref[:, columns], (((1,), (0,)), ((), ())))
    pooled = jnp.concatenate(
        [sums[h * docs : (h + 1) * docs] for h in range(heads)], axis=1
    ) / lens_column(lens_ref, docs)
    emb = exact_dot(pooled, w_ref[...], (((1,), (0,)), ((), ())))
    out_ref[:, : emb.shape[1]] = emb
    out_ref[:, emb.shape[1] :] = by_head[:docs, :]


def pack_kernel(q_ref, out_ref):
    chunks = q_ref.shape[1] // HD
    rows = q_ref[...].astype(jnp.float32)
    rest = jnp.zeros((out_ref.shape[1] - chunks, HD), jnp.float32)
    for k in range(q_ref.shape[0]):
        parts = [rows[k : k + 1, c * HD : (c + 1) * HD] for c in range(chunks)]
        out_ref[k] = jnp.concatenate([*parts, rest], axis=0).astype(jnp.bfloat16)


def copies_kernel(row_ref, out_ref):
    features = 2 * out_ref.shape[2]
    chunks = features // row_ref.shape[0] // HD
    parts = []
    for k in range(row_ref.shape[0]):
        block = row_ref[k].astype(jnp.float32)
        parts += [block[c : c + 1, :] for c in range(chunks)]
    middle = len(parts) // 2
    halves = [jnp.concatenate(parts[:middle], axis=1), jnp.concatenate(parts[middle:], axis=1)]
    both = jnp.concatenate(halves, axis=0).astype(jnp.bfloat16)
    out_ref[...] = jnp.broadcast_to(both[None], out_ref.shape)


def pair_logits(unit, q_ref):
    half = q_ref.shape[1]
    docs = unit.shape[0]
    both = jnp.concatenate([unit[:, :half], unit[:, half:]], axis=0)
    parts = lax.dot_general(both, q_ref[...], NT, preferred_element_type=jnp.float32)
    even = lax.broadcasted_iota(jnp.int32, (docs, q_ref.shape[0]), 1) % 2 == 0
    mine = jnp.where(even, parts[:docs], parts[docs:])
    width = mine.shape[1]
    other = jnp.where(even, pltpu.roll(mine, width - 1, 1), pltpu.roll(mine, 1, 1))
    return sim_scale * (mine + other)


def positive_mask(pos_ref, docs):
    count, classes = pos_ref.shape
    mine = lax.broadcasted_iota(jnp.int32, (count, classes), 1) == lax.axis_index((DP[3], *HEAD))
    lane = lax.broadcasted_iota(jnp.int32, (count, 2 * count), 1)
    row = lax.broadcasted_iota(jnp.int32, (count, 2 * count), 0)
    spread = (lane // 2 == row).astype(jnp.bfloat16)
    pos = jnp.where(mine, pos_ref[...], 0)

    def spread_out(digit):
        lines = lax.dot_general(
            digit.astype(jnp.float32).astype(jnp.bfloat16), spread, TN,
            preferred_element_type=jnp.float32,
        )
        return jnp.sum(lines, axis=0, keepdims=True)

    positive = 128.0 * spread_out(pos // 128) + spread_out(pos % 128)
    owned = lax.axis_index(DP[:3]) * docs + lax.broadcasted_iota(jnp.int32, (docs, 2 * count), 0)
    return (positive == owned.astype(jnp.float32)).astype(jnp.float32)


def logits_kernel(emb_ref, q_ref, pos_ref, out_ref, logits_ref, chosen_ref, unit_ref, rnorm_ref):
    emb = jnp.concatenate([emb_ref[k] for k in range(emb_ref.shape[0])], axis=0)
    rnorm = 1.0 / jnp.sqrt(jnp.sum(emb * emb, axis=1, keepdims=True) + 1e-06)
    unit = emb * rnorm
    logits = pair_logits(unit.astype(jnp.bfloat16), q_ref)
    chosen = positive_mask(pos_ref, emb.shape[0])
    top = jnp.max(logits, axis=0, keepdims=True)
    lse = top + jnp.log(jnp.sum(jnp.exp(logits - top), axis=0, keepdims=True))
    positive = jnp.sum(logits * chosen, axis=0, keepdims=True)
    out_ref[...] = jnp.broadcast_to(
        jnp.concatenate([lse, positive], axis=0)[None], out_ref.shape
    )
    logits_ref[...] = logits
    chosen_ref[...] = chosen
    unit_ref[...] = unit
    rnorm_ref[...] = jnp.broadcast_to(rnorm, rnorm_ref.shape)


def slopes_kernel(stats_ref, logits_ref, chosen_ref, unit_ref, rnorm_ref, q_ref, out_ref):
    pair_docs = logits_ref.shape[0]
    half = q_ref.shape[1]
    features = 2 * half
    split = out_ref.shape[0] // 2
    docs = pair_docs // 2
    each = stats_ref[:, 0, :]
    top = jnp.max(each, axis=0, keepdims=True)
    lse = top + jnp.log(jnp.sum(jnp.exp(each - top), axis=0, keepdims=True))
    positive = jnp.sum(stats_ref[:, 1, :], axis=0, keepdims=True)
    slopes = jnp.exp(logits_ref[...] - lse) - chosen_ref[...]
    even = lax.broadcasted_iota(jnp.int32, slopes.shape, 1) % 2 == 0
    both = jnp.concatenate([jnp.where(even, slopes, 0.0), jnp.where(even, 0.0, slopes)], axis=0)
    parts = sim_scale * exact_dot(both, q_ref[...], (((1,), (0,)), ((), ())))
    grads = jnp.concatenate([parts[:pair_docs], parts[pair_docs:]], axis=1)
    unit = unit_ref[...]
    inner = jnp.sum(unit * grads, axis=1, keepdims=True)
    grads = (rnorm_ref[:, :1] * (grads - unit * inner)).astype(jnp.bfloat16)
    losses = jnp.broadcast_to(lse - positive, (docs, lse.shape[1]))
    row = lax.broadcasted_iota(jnp.int32, losses.shape, 0)
    high = losses.astype(jnp.bfloat16).astype(jnp.float32)
    mid = (losses - high).astype(jnp.bfloat16).astype(jnp.float32)
    losses = jnp.where(row == 0, high, jnp.where(row == 1, mid, losses - high - mid))
    for k in range(2 * split):
        core = k // split
        out_ref[k, :, :features] = grads[core * docs : (core + 1) * docs]
        out_ref[k, :, features:] = losses.astype(jnp.bfloat16)


def values_kernel(
    lens_ref, grads_ref, my_rows_ref, their_rows_ref, my_sums_ref, their_sums_ref, out_ref, loss_ref
):
    docs = lens_ref.shape[1]
    features = my_rows_ref.shape[1]
    seq_len = out_ref.shape[1]
    half = HD // 2
    heads = my_rows_ref.shape[0] // HD
    low = lax.axis_index(HEAD[1])
    grads = grads_ref[0].astype(jnp.float32)
    for k in range(1, grads_ref.shape[0]):
        grads = grads + grads_ref[k].astype(jnp.float32)
    lanes = grads.shape[1] - features
    loss_ref[...] = jnp.sum(
        jnp.sum(grads[:3, features:], axis=0, keepdims=True), axis=1, keepdims=True
    ) / (grads_ref.shape[0] * lanes)
    terms = three_terms(grads[:, :features])
    factor = loss_scale / lens_column(lens_ref, docs)
    slopes = []
    for h in range(heads):
        rows = my_rows_ref[pl.ds(pl.multiple_of(h * HD + low * half, half), half), :]
        slopes.append(lax.dot_general(terms, rows, NT, preferred_element_type=jnp.float32))
    for h in range(heads):
        rows = their_rows_ref[1 - low, h * half : (h + 1) * half, :]
        slopes.append(lax.dot_general(terms, rows, NT, preferred_element_type=jnp.float32))
    slopes = [(of_three(part) * factor).astype(jnp.bfloat16) for part in slopes]
    seg, _ = document_of(lens_ref, docs, (1, seq_len), 1)
    member = lax.broadcasted_iota(jnp.int32, (docs, seq_len), 0) == seg
    shares = []
    for sums in (my_sums_ref, their_sums_ref):
        shares += [jnp.where(member, sums[h : h + 1, features:], 0.0) for h in range(heads)]
    out = lax.dot_general(
        jnp.concatenate(slopes * 3, axis=0),
        three_terms(jnp.concatenate(shares, axis=0)),
        TN,
        preferred_element_type=jnp.float32,
    )
    out_ref[...] = out.astype(jnp.bfloat16)


def per_device(attn_queries, keys, values, out_weight, lengths, queries, positives):
    seq_len, width = attn_queries.shape
    heads = width // HD
    docs = lengths.shape[1]
    features = out_weight.shape[1]
    split = lax.axis_size(HEAD)
    cores = lax.axis_size(DP[3])
    others = lax.axis_size(DP[:3])
    lanes = 2 * others
    f32, bf16 = jnp.float32, jnp.bfloat16
    big = pltpu.CompilerParams(vmem_limit_bytes=60 * 2**20)
    small = pltpu.CompilerParams(vmem_limit_bytes=16 * 2**20)

    half = HD // 2
    low = lax.axis_index(HEAD[1])
    rows_of = out_weight.reshape(heads, 2, half, features)
    wanted = lax.dynamic_index_in_dim(rows_of, 1 - low, 1, keepdims=False)
    their_rows = lax.all_gather(wanted.reshape(heads * half, features), HEAD[1])

    row = pl.pallas_call(
        pack_kernel,
        out_shape=jax.ShapeDtypeStruct((split, 16, HD), bf16),
        in_specs=[VMEM],
        out_specs=VMEM,
        compiler_params=small,
        name="pack",
    )(queries)
    row = lax.all_to_all(row, HEAD, 0, 0, tiled=True)
    partial = pl.pallas_call(
        attend_kernel,
        out_shape=jax.ShapeDtypeStruct((docs, features + seq_len), f32),
        in_specs=[SMEM] + [VMEM] * 4,
        out_specs=VMEM,
        scratch_shapes=[pltpu.VMEM((seq_len, HD), f32)],
        compiler_params=big,
        name="attend",
    )(lengths, attn_queries, keys, values, out_weight)
    row, partial = lax.optimization_barrier((row, partial))
    rows = pl.pallas_call(
        copies_kernel,
        out_shape=jax.ShapeDtypeStruct((others, 2, features // 2), bf16),
        in_specs=[VMEM],
        out_specs=VMEM,
        compiler_params=small,
        name="copies",
    )(row)
    every = lax.all_to_all(rows, DP[:3], 0, 0, tiled=True).reshape(lanes, features // 2)
    pos = positives.reshape(others, cores * split)

    theirs = lax.ppermute(partial, HEAD, [(i, i ^ 1) for i in range(split)])
    emb = partial[:, :features]
    whole = emb + theirs[:, :features]
    for apart in range(2, split):
        whole = whole + lax.ppermute(emb, HEAD, [(i, i ^ apart) for i in range(split)])
    pair = lax.all_gather(whole, DP[3])

    stats, logits, chosen, unit, rnorm = pl.pallas_call(
        logits_kernel,
        out_shape=(
            jax.ShapeDtypeStruct((others, 2, lanes), f32),
            jax.ShapeDtypeStruct((cores * docs, lanes), f32),
            jax.ShapeDtypeStruct((cores * docs, lanes), f32),
            jax.ShapeDtypeStruct((cores * docs, features), f32),
            jax.ShapeDtypeStruct((cores * docs, HD), f32),
        ),
        in_specs=[VMEM] * 3,
        out_specs=(VMEM,) * 5,
        compiler_params=small,
        name="logits",
    )(pair, every, pos)
    stats = lax.all_to_all(stats, DP[:3], 0, 0, tiled=True)
    stats, their_rows = lax.optimization_barrier((stats, their_rows))

    grads = pl.pallas_call(
        slopes_kernel,
        out_shape=jax.ShapeDtypeStruct((cores * split, docs, features + lanes), bf16),
        in_specs=[VMEM] * 6,
        out_specs=VMEM,
        compiler_params=small,
        name="slopes",
    )(stats, logits, chosen, unit, rnorm, every)
    grads = lax.all_to_all(grads, (DP[3], *HEAD), 0, 0, tiled=True)

    d_values, loss = pl.pallas_call(
        values_kernel,
        out_shape=(
            jax.ShapeDtypeStruct((half, seq_len), bf16),
            jax.ShapeDtypeStruct((1, 1), f32),
        ),
        in_specs=[SMEM] + [VMEM] * 5,
        out_specs=(VMEM, VMEM),
        compiler_params=small,
        name="slopes_of_values",
    )(lengths, grads, out_weight, their_rows, partial, theirs)
    return d_values.T, loss.reshape(())


def solution(mesh):
    shape = (4, 8, 2, 2) if mesh.devices.size == 512 else (1, mesh.devices.size // 16, 2, 2)
    head = mesh.shape["head"]
    torus = Mesh(mesh.devices.reshape(*shape, head // 2, 2), (*DP, *HEAD))
    placed = (
        P(DP, HEAD),
        P(DP, None),
        P(DP, None),
        P(HEAD, None),
        P(DP, None),
        P(DP, HEAD),
        P(),
    )
    return jax.shard_map(
        per_device, mesh=torus, in_specs=placed, out_specs=(P(DP, HEAD), P()), check_vma=False
    )
```

```python
import math

import jax
import jax.numpy as jnp
from jax import lax
from jax.experimental import pallas as pl
from jax.experimental.pallas import tpu as pltpu
from jax.sharding import Mesh
from jax.sharding import PartitionSpec as P

HEADS = 12
KV_HEADS = 2
HD = 128
DP = ("dp_0", "dp_1", "dp_2", "dp_3")
LONGEST = 256
HEAD = ("head_0", "head_1")

sim_scale = 20.0
loss_scale = 32768.0

NT = (((1,), (1,)), ((), ()))
TN = (((0,), (0,)), ((), ()))
VMEM = pl.BlockSpec(memory_space=pltpu.VMEM)
SMEM = pl.BlockSpec(memory_space=pltpu.SMEM)


def query_class():
    return lax.axis_index(HEAD) ^ (2 * lax.axis_index(DP[2]))


def class_groups():
    split, uppers = lax.axis_size(HEAD), lax.axis_size(DP[2])
    blocks = lax.axis_size(DP[:2])
    return [
        [(b * uppers + u) * split + (k ^ (2 * u)) for b in range(blocks) for u in range(uppers)]
        for k in range(split)
    ]


def three_terms(value):
    high = value.astype(jnp.bfloat16)
    rest = value - high.astype(jnp.float32)
    mid = rest.astype(jnp.bfloat16)
    low = (rest - mid.astype(jnp.float32)).astype(jnp.bfloat16)
    return jnp.concatenate([high, mid, low], axis=0)


def of_three(value):
    rows = value.shape[0] // 3
    return value[:rows] + value[rows : 2 * rows] + value[2 * rows :]


def exact_dot(value, other, dims):
    return of_three(
        lax.dot_general(three_terms(value), other, dims, preferred_element_type=jnp.float32)
    )


def document_of(lens_ref, docs, shape, dim):
    place = lax.broadcasted_iota(jnp.int32, shape, dim)
    seg = jnp.zeros(shape, jnp.int32)
    start = jnp.zeros(shape, jnp.int32)
    end = jnp.int32(0)
    for j in range(docs):
        end = end + lens_ref[0, j]
        past = place >= end
        seg = seg + past.astype(jnp.int32)
        start = jnp.where(past, end, start)
    return seg, start


def lens_column(lens_ref, docs):
    row = lax.broadcasted_iota(jnp.int32, (docs, 1), 0)
    column = jnp.zeros((docs, 1), jnp.int32)
    for j in range(docs):
        column = jnp.where(row == j, lens_ref[0, j], column)
    return column.astype(jnp.float32)


def attend_kernel(
    lens_ref, q_ref, k_ref, v_ref, w_ref, queries_ref, *out_refs
):
    *sent_refs, rows_ref, total = out_refs
    seq_len, width = q_ref.shape
    heads = width // HD
    docs = lens_ref.shape[1]
    kv_head = lax.axis_index(HEAD) * heads // (HEADS // KV_HEADS)
    columns = pl.ds(pl.multiple_of(kv_head * HD, HD), HD)
    seg, start = document_of(lens_ref, docs, (1, seq_len), 1)
    total[...] = jnp.zeros_like(total)
    block = min(128, seq_len)
    factor = math.log2(math.e) / math.sqrt(HD)
    lane = lax.broadcasted_iota(jnp.int32, (block, HD), 1)
    for first in range(0, seq_len, block):
        low = max(0, (first - LONGEST + 1) // block * block)
        span = first + block - low
        k_block = k_ref[low : first + block, columns]
        k_place = low + lax.broadcasted_iota(jnp.int32, (span, block), 0)
        q_place = first + lax.broadcasted_iota(jnp.int32, (span, block), 1)
        allowed = (k_place <= q_place) & (k_place >= start[:, first : first + block])
        for h in range(heads):
            q_block = q_ref[first : first + block, h * HD : (h + 1) * HD]
            scores = lax.dot_general(k_block, q_block, NT, preferred_element_type=jnp.float32)
            scores = jnp.where(allowed, scores, -1e30)
            top = jnp.max(scores, axis=0, keepdims=True)
            expo = jnp.exp2((scores - top) * factor)
            norm = 1.0 / jnp.sum(expo, axis=0, keepdims=True)
            probs = (expo * norm).astype(jnp.bfloat16)
            pick = (lane == h).astype(jnp.bfloat16)
            total[low : first + block, :] += jnp.dot(
                probs, pick, preferred_element_type=jnp.float32
            )
    by_head = total[...].T
    member = lax.broadcasted_iota(jnp.int32, (docs, seq_len), 0) == seg
    shares = jnp.concatenate(
        [jnp.where(member, by_head[h : h + 1, :], 0.0) for h in range(heads)], axis=0
    )
    sums = exact_dot(shares, v_ref[:, columns], (((1,), (0,)), ((), ())))
    pooled = jnp.concatenate(
        [sums[h * docs : (h + 1) * docs] for h in range(heads)], axis=1
    ) / lens_column(lens_ref, docs)
    emb = exact_dot(pooled, w_ref[...], (((1,), (0,)), ((), ())))
    features = emb.shape[1]
    queries = queries_ref[...].astype(jnp.float32)
    place = lax.broadcasted_iota(jnp.int32, queries.shape, 0)
    rest = jnp.zeros((docs - heads - 1, seq_len), jnp.float32)
    tail = jnp.zeros((1, seq_len - width), jnp.float32)
    for apart, sent_ref in enumerate(sent_refs):
        row = jnp.where(place == (query_class() ^ apart), queries, 0.0)
        row = jnp.concatenate([jnp.sum(row, axis=0, keepdims=True), tail], axis=1)
        sent_ref[:, :features] = emb
        sent_ref[:, features:] = jnp.concatenate([by_head[:heads], row, rest], axis=0)
    half = HD // 2
    for h in range(heads):
        wanted = pl.ds(pl.multiple_of(h * HD + (1 - lax.axis_index(HEAD[1])) * half, half), half)
        rows_ref[h * half : (h + 1) * half, :] = w_ref[wanted, :]


def copies_kernel(*refs):
    *partial_refs, out_ref, whole_ref = refs
    docs, features = whole_ref.shape
    split = len(partial_refs)
    width = features // split
    row = HEADS // split
    me = lax.axis_index(HEAD)
    slices = [ref[row : row + 1, features : features + width] for ref in partial_refs]
    parts = []
    for owner in range(split):
        part = jnp.zeros_like(slices[0])
        for apart in range(split):
            part = jnp.where(me == owner ^ apart, slices[apart], part)
        parts.append(part)
    middle = split // 2
    halves = [jnp.concatenate(parts[:middle], axis=1), jnp.concatenate(parts[middle:], axis=1)]
    both = jnp.concatenate(halves, axis=0).astype(jnp.bfloat16)
    out_ref[...] = jnp.broadcast_to(both[None], out_ref.shape)
    whole = partial_refs[0][:, :features]
    for ref in partial_refs[1:]:
        whole = whole + ref[:, :features]
    whole_ref[...] = whole


def pair_logits(unit, q_ref):
    half = q_ref.shape[1]
    docs = unit.shape[0]
    both = jnp.concatenate([unit[:, :half], unit[:, half:]], axis=0)
    parts = lax.dot_general(both, q_ref[...], NT, preferred_element_type=jnp.float32)
    even = lax.broadcasted_iota(jnp.int32, (docs, q_ref.shape[0]), 1) % 2 == 0
    mine = jnp.where(even, parts[:docs], parts[docs:])
    width = mine.shape[1]
    other = jnp.where(even, pltpu.roll(mine, width - 1, 1), pltpu.roll(mine, 1, 1))
    return sim_scale * (mine + other)


def positive_mask(pos_ref, docs):
    count, classes = pos_ref.shape
    mine = lax.broadcasted_iota(jnp.int32, (count, classes), 1) == (
        lax.axis_size(HEAD) * lax.axis_index(DP[3]) + query_class()
    )
    lane = lax.broadcasted_iota(jnp.int32, (count, 2 * count), 1)
    row = lax.broadcasted_iota(jnp.int32, (count, 2 * count), 0)
    spread = (lane // 2 == row).astype(jnp.bfloat16)
    pos = jnp.where(mine, pos_ref[...], 0)

    def spread_out(digit):
        lines = lax.dot_general(
            digit.astype(jnp.float32).astype(jnp.bfloat16), spread, TN,
            preferred_element_type=jnp.float32,
        )
        return jnp.sum(lines, axis=0, keepdims=True)

    positive = 128.0 * spread_out(pos // 128) + spread_out(pos % 128)
    owned = lax.axis_index(DP[:3]) * docs + lax.broadcasted_iota(jnp.int32, (docs, 2 * count), 0)
    return (positive == owned.astype(jnp.float32)).astype(jnp.float32)


def logits_kernel(emb_ref, q_ref, pos_ref, out_ref, logits_ref, chosen_ref, unit_ref, rnorm_ref):
    emb = jnp.concatenate([emb_ref[k] for k in range(emb_ref.shape[0])], axis=0)
    rnorm = 1.0 / jnp.sqrt(jnp.sum(emb * emb, axis=1, keepdims=True) + 1e-06)
    unit = emb * rnorm
    logits = pair_logits(unit.astype(jnp.bfloat16), q_ref)
    chosen = positive_mask(pos_ref, emb.shape[0])
    top = jnp.max(logits, axis=0, keepdims=True)
    lse = top + jnp.log(jnp.sum(jnp.exp(logits - top), axis=0, keepdims=True))
    positive = jnp.sum(logits * chosen, axis=0, keepdims=True)
    out_ref[...] = jnp.broadcast_to(
        jnp.concatenate([lse, positive], axis=0)[None], out_ref.shape
    )
    logits_ref[...] = logits
    chosen_ref[...] = chosen
    unit_ref[...] = unit
    rnorm_ref[...] = jnp.broadcast_to(rnorm, rnorm_ref.shape)


def slopes_kernel(stats_ref, logits_ref, chosen_ref, unit_ref, rnorm_ref, q_ref, out_ref):
    pair_docs = logits_ref.shape[0]
    half = q_ref.shape[1]
    features = 2 * half
    split = out_ref.shape[0] // 2
    docs = pair_docs // 2
    each = stats_ref[:, 0, :]
    top = jnp.max(each, axis=0, keepdims=True)
    lse = top + jnp.log(jnp.sum(jnp.exp(each - top), axis=0, keepdims=True))
    positive = jnp.sum(stats_ref[:, 1, :], axis=0, keepdims=True)
    slopes = jnp.exp(logits_ref[...] - lse) - chosen_ref[...]
    even = lax.broadcasted_iota(jnp.int32, slopes.shape, 1) % 2 == 0
    both = jnp.concatenate([jnp.where(even, slopes, 0.0), jnp.where(even, 0.0, slopes)], axis=0)
    parts = sim_scale * exact_dot(both, q_ref[...], (((1,), (0,)), ((), ())))
    grads = jnp.concatenate([parts[:pair_docs], parts[pair_docs:]], axis=1)
    unit = unit_ref[...]
    inner = jnp.sum(unit * grads, axis=1, keepdims=True)
    grads = (rnorm_ref[:, :1] * (grads - unit * inner)).astype(jnp.bfloat16)
    losses = jnp.broadcast_to(lse - positive, (docs, lse.shape[1]))
    row = lax.broadcasted_iota(jnp.int32, losses.shape, 0)
    high = losses.astype(jnp.bfloat16).astype(jnp.float32)
    mid = (losses - high).astype(jnp.bfloat16).astype(jnp.float32)
    losses = jnp.where(row == 0, high, jnp.where(row == 1, mid, losses - high - mid))
    for k in range(2 * split):
        core = k // split
        out_ref[k, :, :features] = grads[core * docs : (core + 1) * docs]
        out_ref[k, :, features:] = losses.astype(jnp.bfloat16)


def values_kernel(
    lens_ref, grads_ref, my_rows_ref, their_rows_ref, my_sums_ref, their_sums_ref, out_ref, loss_ref
):
    docs = lens_ref.shape[1]
    features = my_rows_ref.shape[1]
    seq_len = out_ref.shape[1]
    half = HD // 2
    heads = my_rows_ref.shape[0] // HD
    low = lax.axis_index(HEAD[1])
    grads = grads_ref[0].astype(jnp.float32)
    for k in range(1, grads_ref.shape[0]):
        grads = grads + grads_ref[k].astype(jnp.float32)
    lanes = grads.shape[1] - features
    loss_ref[...] = jnp.sum(
        jnp.sum(grads[:3, features:], axis=0, keepdims=True), axis=1, keepdims=True
    ) / (grads_ref.shape[0] * lanes)
    terms = three_terms(grads[:, :features])
    factor = loss_scale / lens_column(lens_ref, docs)
    slopes = []
    for h in range(heads):
        rows = my_rows_ref[pl.ds(pl.multiple_of(h * HD + low * half, half), half), :]
        slopes.append(lax.dot_general(terms, rows, NT, preferred_element_type=jnp.float32))
    for h in range(heads):
        rows = their_rows_ref[h * half : (h + 1) * half, :]
        slopes.append(lax.dot_general(terms, rows, NT, preferred_element_type=jnp.float32))
    slopes = [(of_three(part) * factor).astype(jnp.bfloat16) for part in slopes]
    seg, _ = document_of(lens_ref, docs, (1, seq_len), 1)
    member = lax.broadcasted_iota(jnp.int32, (docs, seq_len), 0) == seg
    shares = []
    for sums in (my_sums_ref, their_sums_ref):
        shares += [jnp.where(member, sums[h : h + 1, features:], 0.0) for h in range(heads)]
    out = lax.dot_general(
        jnp.concatenate(slopes * 3, axis=0),
        three_terms(jnp.concatenate(shares, axis=0)),
        TN,
        preferred_element_type=jnp.float32,
    )
    out_ref[...] = out.astype(jnp.bfloat16)


def per_device(attn_queries, keys, values, out_weight, lengths, queries, positives):
    seq_len, width = attn_queries.shape
    heads = width // HD
    docs = lengths.shape[1]
    features = out_weight.shape[1]
    split = lax.axis_size(HEAD)
    cores = lax.axis_size(DP[3])
    others = lax.axis_size(DP[:3])
    lanes = 2 * others
    f32, bf16 = jnp.float32, jnp.bfloat16
    big = pltpu.CompilerParams(vmem_limit_bytes=60 * 2**20)
    small = pltpu.CompilerParams(vmem_limit_bytes=16 * 2**20)

    half = HD // 2
    line = (*DP[:3], *HEAD)
    groups = class_groups()
    pairs = [[(i, i ^ apart) for i in range(split)] for apart in range(split)]

    *partials, wanted = pl.pallas_call(
        attend_kernel,
        out_shape=(jax.ShapeDtypeStruct((docs, features + seq_len), f32),) * split
        + (jax.ShapeDtypeStruct((heads * half, features), bf16),),
        in_specs=[SMEM] + [VMEM] * 5,
        out_specs=(VMEM,) * (split + 1),
        scratch_shapes=[pltpu.VMEM((seq_len, HD), f32)],
        compiler_params=big,
        name="attend",
    )(lengths, attn_queries, keys, values, out_weight, queries)
    own = partials[0]
    got = [lax.ppermute(partials[apart], HEAD, pairs[apart]) for apart in range(1, split)]
    their_rows = lax.ppermute(wanted, HEAD, pairs[1])
    rows, whole = pl.pallas_call(
        copies_kernel,
        out_shape=(
            jax.ShapeDtypeStruct((others, 2, features // 2), bf16),
            jax.ShapeDtypeStruct((docs, features), f32),
        ),
        in_specs=[VMEM] * split,
        out_specs=(VMEM, VMEM),
        compiler_params=small,
        name="copies",
    )(own, *got)
    every = lax.all_to_all(rows, line, 0, 0, axis_index_groups=groups, tiled=True)
    every = every.reshape(lanes, features // 2)
    pos = positives.reshape(others, cores * split)
    pair = lax.all_gather(whole, DP[3])

    stats, logits, chosen, unit, rnorm = pl.pallas_call(
        logits_kernel,
        out_shape=(
            jax.ShapeDtypeStruct((others, 2, lanes), f32),
            jax.ShapeDtypeStruct((cores * docs, lanes), f32),
            jax.ShapeDtypeStruct((cores * docs, lanes), f32),
            jax.ShapeDtypeStruct((cores * docs, features), f32),
            jax.ShapeDtypeStruct((cores * docs, HD), f32),
        ),
        in_specs=[VMEM] * 3,
        out_specs=(VMEM,) * 5,
        compiler_params=small,
        name="logits",
    )(pair, every, pos)
    stats = lax.all_to_all(stats, line, 0, 0, axis_index_groups=groups, tiled=True)

    grads = pl.pallas_call(
        slopes_kernel,
        out_shape=jax.ShapeDtypeStruct((cores * split, docs, features + lanes), bf16),
        in_specs=[VMEM] * 6,
        out_specs=VMEM,
        compiler_params=small,
        name="slopes",
    )(stats, logits, chosen, unit, rnorm, every)
    grads = lax.all_to_all(grads, (DP[3], *HEAD), 0, 0, tiled=True)

    d_values, loss = pl.pallas_call(
        values_kernel,
        out_shape=(
            jax.ShapeDtypeStruct((half, seq_len), bf16),
            jax.ShapeDtypeStruct((1, 1), f32),
        ),
        in_specs=[SMEM] + [VMEM] * 5,
        out_specs=(VMEM, VMEM),
        compiler_params=small,
        name="slopes_of_values",
    )(lengths, grads, out_weight, their_rows, own, got[0])
    return d_values.T, loss.reshape(())


def solution(mesh):
    shape = (4, 8, 2, 2) if mesh.devices.size == 512 else (1, mesh.devices.size // 16, 2, 2)
    head = mesh.shape["head"]
    torus = Mesh(mesh.devices.reshape(*shape, head // 2, 2), (*DP, *HEAD))
    placed = (
        P(DP, HEAD),
        P(DP, None),
        P(DP, None),
        P(HEAD, None),
        P(DP, None),
        P(DP, HEAD),
        P(),
    )
    return jax.shard_map(
        per_device, mesh=torus, in_specs=placed, out_specs=(P(DP, HEAD), P()), check_vma=False
    )
```

```python
import math

import jax
import jax.numpy as jnp
from jax import lax
from jax.experimental import pallas as pl
from jax.experimental.pallas import tpu as pltpu
from jax.sharding import Mesh
from jax.sharding import PartitionSpec as P

HEADS = 12
KV_HEADS = 2
HD = 128
DP = ("dp_0", "dp_1", "dp_2", "dp_3")
LONGEST = 256
HEAD = ("head_0", "head_1")

sim_scale = 20.0
loss_scale = 32768.0

NT = (((1,), (1,)), ((), ()))
TN = (((0,), (0,)), ((), ()))
VMEM = pl.BlockSpec(memory_space=pltpu.VMEM)
HBM = pl.BlockSpec(memory_space=pl.ANY)
SMEM = pl.BlockSpec(memory_space=pltpu.SMEM)


def query_class():
    return lax.axis_index(HEAD) ^ (2 * lax.axis_index(DP[2]))


def class_groups():
    split, uppers = lax.axis_size(HEAD), lax.axis_size(DP[2])
    blocks = lax.axis_size(DP[:2])
    return [
        [(b * uppers + u) * split + (k ^ (2 * u)) for b in range(blocks) for u in range(uppers)]
        for k in range(split)
    ]


def three_terms(value):
    high = value.astype(jnp.bfloat16)
    rest = value - high.astype(jnp.float32)
    mid = rest.astype(jnp.bfloat16)
    low = (rest - mid.astype(jnp.float32)).astype(jnp.bfloat16)
    return jnp.concatenate([high, mid, low], axis=0)


def of_three(value):
    rows = value.shape[0] // 3
    return value[:rows] + value[rows : 2 * rows] + value[2 * rows :]


def exact_dot(value, other, dims):
    return of_three(
        lax.dot_general(three_terms(value), other, dims, preferred_element_type=jnp.float32)
    )


def document_of(lens_ref, docs, shape, dim):
    place = lax.broadcasted_iota(jnp.int32, shape, dim)
    seg = jnp.zeros(shape, jnp.int32)
    start = jnp.zeros(shape, jnp.int32)
    end = jnp.int32(0)
    for j in range(docs):
        end = end + lens_ref[0, j]
        past = place >= end
        seg = seg + past.astype(jnp.int32)
        start = jnp.where(past, end, start)
    return seg, start


def lens_column(lens_ref, docs):
    row = lax.broadcasted_iota(jnp.int32, (docs, 1), 0)
    column = jnp.zeros((docs, 1), jnp.int32)
    for j in range(docs):
        column = jnp.where(row == j, lens_ref[0, j], column)
    return column.astype(jnp.float32)


def attend_kernel(
    lens_ref, q_hbm, k_hbm, v_hbm, w_hbm, queries_ref, sent_ref, rows_ref,
    q_ref, k_ref, v_ref, w_ref, total, done,
):
    copies = [
        pltpu.make_async_copy(source, target, done.at[i])
        for i, (source, target) in enumerate(
            ((q_hbm, q_ref), (k_hbm, k_ref), (v_hbm, v_ref), (w_hbm, w_ref))
        )
    ]
    for copy in copies:
        copy.start()
    seq_len, width = q_ref.shape
    heads = width // HD
    docs = lens_ref.shape[1]
    kv_head = lax.axis_index(HEAD) * heads // (HEADS // KV_HEADS)
    columns = pl.ds(pl.multiple_of(kv_head * HD, HD), HD)
    seg, start = document_of(lens_ref, docs, (1, seq_len), 1)
    total[...] = jnp.zeros_like(total)
    block = min(128, seq_len)
    factor = math.log2(math.e) / math.sqrt(HD)
    lane = lax.broadcasted_iota(jnp.int32, (block, HD), 1)
    copies[0].wait()
    copies[1].wait()
    for first in range(0, seq_len, block):
        low = max(0, (first - LONGEST + 1) // block * block)
        span = first + block - low
        k_block = k_ref[low : first + block, columns]
        k_place = low + lax.broadcasted_iota(jnp.int32, (span, block), 0)
        q_place = first + lax.broadcasted_iota(jnp.int32, (span, block), 1)
        allowed = (k_place <= q_place) & (k_place >= start[:, first : first + block])
        for h in range(heads):
            q_block = q_ref[first : first + block, h * HD : (h + 1) * HD]
            scores = lax.dot_general(k_block, q_block, NT, preferred_element_type=jnp.float32)
            scores = jnp.where(allowed, scores, -1e30)
            top = jnp.max(scores, axis=0, keepdims=True)
            expo = jnp.exp2((scores - top) * factor)
            norm = 1.0 / jnp.sum(expo, axis=0, keepdims=True)
            probs = (expo * norm).astype(jnp.bfloat16)
            pick = (lane == h).astype(jnp.bfloat16)
            total[low : first + block, :] += jnp.dot(
                probs, pick, preferred_element_type=jnp.float32
            )
    by_head = total[...].T
    member = lax.broadcasted_iota(jnp.int32, (docs, seq_len), 0) == seg
    shares = jnp.concatenate(
        [jnp.where(member, by_head[h : h + 1, :], 0.0) for h in range(heads)], axis=0
    )
    copies[2].wait()
    sums = exact_dot(shares, v_ref[:, columns], (((1,), (0,)), ((), ())))
    pooled = jnp.concatenate(
        [sums[h * docs : (h + 1) * docs] for h in range(heads)], axis=1
    ) / lens_column(lens_ref, docs)
    copies[3].wait()
    emb = exact_dot(pooled, w_ref[...], (((1,), (0,)), ((), ())))
    features = emb.shape[1]
    queries = queries_ref[...].astype(jnp.float32)
    place = lax.broadcasted_iota(jnp.int32, queries.shape, 0)
    middle = seq_len // 2
    pad = jnp.zeros((1, 2 * middle - width), jnp.float32)
    for k in range(sent_ref.shape[0]):
        row = jnp.where(place == k ^ (2 * lax.axis_index(DP[2])), queries, 0.0)
        row = jnp.sum(row, axis=0, keepdims=True)
        sent_ref[k, :, :features] = emb
        sent_ref[k, :, features:] = jnp.concatenate(
            [
                by_head[:heads, :middle],
                by_head[:heads, middle:],
                row[:, :middle],
                jnp.concatenate([row[:, middle:], pad], axis=1),
            ],
            axis=0,
        )
    half = HD // 2
    for h in range(heads):
        wanted = pl.ds(pl.multiple_of(h * HD + (1 - lax.axis_index(HEAD[1])) * half, half), half)
        rows_ref[h * half : (h + 1) * half, :] = w_ref[wanted, :]


def copies_kernel(got_ref, out_ref, whole_ref):
    docs, features = whole_ref.shape
    split = got_ref.shape[0]
    width = features // split
    place = 2 * (HEADS // split)
    parts = []
    for k in range(split):
        line = got_ref[k, place:, features:]
        middle = line.shape[1]
        parts += [line[:1, :], line[1:, : width - middle]]
    middle = split
    halves = [jnp.concatenate(parts[:middle], axis=1), jnp.concatenate(parts[middle:], axis=1)]
    both = jnp.concatenate(halves, axis=0).astype(jnp.bfloat16)
    out_ref[...] = jnp.broadcast_to(both[None], out_ref.shape)
    whole = got_ref[0, :, :features]
    for k in range(1, split):
        whole = whole + got_ref[k, :, :features]
    whole_ref[...] = whole


def pair_logits(unit, q_ref):
    half = q_ref.shape[1]
    docs = unit.shape[0]
    both = jnp.concatenate([unit[:, :half], unit[:, half:]], axis=0)
    parts = lax.dot_general(both, q_ref[...], NT, preferred_element_type=jnp.float32)
    even = lax.broadcasted_iota(jnp.int32, (docs, q_ref.shape[0]), 1) % 2 == 0
    mine = jnp.where(even, parts[:docs], parts[docs:])
    width = mine.shape[1]
    other = jnp.where(even, pltpu.roll(mine, width - 1, 1), pltpu.roll(mine, 1, 1))
    return sim_scale * (mine + other)


def positive_mask(pos_ref, docs):
    count, classes = pos_ref.shape
    mine = lax.broadcasted_iota(jnp.int32, (count, classes), 1) == (
        lax.axis_size(HEAD) * lax.axis_index(DP[3]) + query_class()
    )
    lane = lax.broadcasted_iota(jnp.int32, (count, 2 * count), 1)
    row = lax.broadcasted_iota(jnp.int32, (count, 2 * count), 0)
    spread = (lane // 2 == row).astype(jnp.bfloat16)
    pos = jnp.where(mine, pos_ref[...], 0)

    def spread_out(digit):
        lines = lax.dot_general(
            digit.astype(jnp.float32).astype(jnp.bfloat16), spread, TN,
            preferred_element_type=jnp.float32,
        )
        return jnp.sum(lines, axis=0, keepdims=True)

    positive = 128.0 * spread_out(pos // 128) + spread_out(pos % 128)
    owned = lax.axis_index(DP[:3]) * docs + lax.broadcasted_iota(jnp.int32, (docs, 2 * count), 0)
    return (positive == owned.astype(jnp.float32)).astype(jnp.float32)


def logits_kernel(emb_ref, q_ref, pos_ref, out_ref, logits_ref, chosen_ref, unit_ref, rnorm_ref):
    emb = jnp.concatenate([emb_ref[k] for k in range(emb_ref.shape[0])], axis=0)
    rnorm = 1.0 / jnp.sqrt(jnp.sum(emb * emb, axis=1, keepdims=True) + 1e-06)
    unit = emb * rnorm
    logits = pair_logits(unit.astype(jnp.bfloat16), q_ref)
    chosen = positive_mask(pos_ref, emb.shape[0])
    top = jnp.max(logits, axis=0, keepdims=True)
    lse = top + jnp.log(jnp.sum(jnp.exp(logits - top), axis=0, keepdims=True))
    positive = jnp.sum(logits * chosen, axis=0, keepdims=True)
    out_ref[...] = jnp.broadcast_to(
        jnp.concatenate([lse, positive], axis=0)[None], out_ref.shape
    )
    logits_ref[...] = logits
    chosen_ref[...] = chosen
    unit_ref[...] = unit
    rnorm_ref[...] = jnp.broadcast_to(rnorm, rnorm_ref.shape)


def slopes_kernel(stats_ref, logits_ref, chosen_ref, unit_ref, rnorm_ref, q_ref, out_ref):
    pair_docs = logits_ref.shape[0]
    half = q_ref.shape[1]
    features = 2 * half
    split = out_ref.shape[0] // 2
    docs = pair_docs // 2
    each = stats_ref[:, 0, :]
    top = jnp.max(each, axis=0, keepdims=True)
    lse = top + jnp.log(jnp.sum(jnp.exp(each - top), axis=0, keepdims=True))
    positive = jnp.sum(stats_ref[:, 1, :], axis=0, keepdims=True)
    slopes = jnp.exp(logits_ref[...] - lse) - chosen_ref[...]
    even = lax.broadcasted_iota(jnp.int32, slopes.shape, 1) % 2 == 0
    both = jnp.concatenate([jnp.where(even, slopes, 0.0), jnp.where(even, 0.0, slopes)], axis=0)
    parts = sim_scale * exact_dot(both, q_ref[...], (((1,), (0,)), ((), ())))
    grads = jnp.concatenate([parts[:pair_docs], parts[pair_docs:]], axis=1)
    unit = unit_ref[...]
    inner = jnp.sum(unit * grads, axis=1, keepdims=True)
    grads = (rnorm_ref[:, :1] * (grads - unit * inner)).astype(jnp.bfloat16)
    losses = jnp.broadcast_to(lse - positive, (docs, lse.shape[1]))
    row = lax.broadcasted_iota(jnp.int32, losses.shape, 0)
    high = losses.astype(jnp.bfloat16).astype(jnp.float32)
    mid = (losses - high).astype(jnp.bfloat16).astype(jnp.float32)
    losses = jnp.where(row == 0, high, jnp.where(row == 1, mid, losses - high - mid))
    for k in range(2 * split):
        core = k // split
        out_ref[k, :, :features] = grads[core * docs : (core + 1) * docs]
        out_ref[k, :, features:] = losses.astype(jnp.bfloat16)


def values_kernel(lens_ref, grads_ref, my_rows_ref, their_rows_ref, got_ref, out_ref, loss_ref):
    docs = lens_ref.shape[1]
    features = my_rows_ref.shape[1]
    seq_len = out_ref.shape[1]
    half = HD // 2
    heads = my_rows_ref.shape[0] // HD
    low = lax.axis_index(HEAD[1])
    grads = grads_ref[0].astype(jnp.float32)
    for k in range(1, grads_ref.shape[0]):
        grads = grads + grads_ref[k].astype(jnp.float32)
    lanes = grads.shape[1] - features
    loss_ref[...] = jnp.sum(
        jnp.sum(grads[:3, features:], axis=0, keepdims=True), axis=1, keepdims=True
    ) / (grads_ref.shape[0] * lanes)
    rows = [
        my_rows_ref[pl.ds(pl.multiple_of(h * HD + low * half, half), half), :]
        for h in range(heads)
    ]
    rows = jnp.concatenate([*rows, their_rows_ref[...]], axis=0)
    terms = three_terms(grads[:, :features])
    slopes = lax.dot_general(rows, terms, NT, preferred_element_type=jnp.float32)
    slopes = slopes[:, :docs] + slopes[:, docs : 2 * docs] + slopes[:, 2 * docs :]
    lane = lax.broadcasted_iota(jnp.int32, (1, docs), 1)
    lens = jnp.zeros((1, docs), jnp.int32)
    for j in range(docs):
        lens = jnp.where(lane == j, lens_ref[0, j], lens)
    slopes = (slopes / lens.astype(jnp.float32) * loss_scale).astype(jnp.bfloat16)
    slopes = [slopes[h * half : (h + 1) * half] for h in range(2 * heads)]
    seg, _ = document_of(lens_ref, docs, (1, seq_len), 1)
    member = lax.broadcasted_iota(jnp.int32, (docs, seq_len), 0) == seg
    me = lax.axis_index(HEAD)
    shares = []
    for owner in (me, me ^ 1):
        sums = got_ref[owner, :, features:]
        sums = jnp.concatenate([sums[:heads], sums[heads : 2 * heads]], axis=1)
        shares += [jnp.where(member, sums[h : h + 1], 0.0) for h in range(heads)]
    out = jnp.dot(
        jnp.concatenate(slopes * 3, axis=1),
        three_terms(jnp.concatenate(shares, axis=0)),
        preferred_element_type=jnp.float32,
    )
    out_ref[...] = out.astype(jnp.bfloat16)


def per_device(attn_queries, keys, values, out_weight, lengths, queries, positives):
    seq_len, width = attn_queries.shape
    heads = width // HD
    docs = lengths.shape[1]
    features = out_weight.shape[1]
    split = lax.axis_size(HEAD)
    cores = lax.axis_size(DP[3])
    others = lax.axis_size(DP[:3])
    lanes = 2 * others
    f32, bf16 = jnp.float32, jnp.bfloat16
    big = pltpu.CompilerParams(vmem_limit_bytes=60 * 2**20)
    small = pltpu.CompilerParams(vmem_limit_bytes=16 * 2**20)

    half = HD // 2
    line = (*DP[:3], *HEAD)
    groups = class_groups()

    partial, wanted = pl.pallas_call(
        attend_kernel,
        out_shape=(
            jax.ShapeDtypeStruct((split, docs, features + seq_len // 2), f32),
            jax.ShapeDtypeStruct((heads * half, features), bf16),
        ),
        in_specs=[SMEM] + [HBM] * 4 + [VMEM],
        out_specs=(VMEM, VMEM),
        scratch_shapes=[
            *(pltpu.VMEM(a.shape, a.dtype) for a in (attn_queries, keys, values, out_weight)),
            pltpu.VMEM((seq_len, HD), f32),
            pltpu.SemaphoreType.DMA((4,)),
        ],
        compiler_params=big,
        name="attend",
    )(lengths, attn_queries, keys, values, out_weight, queries)
    got = lax.all_to_all(partial, HEAD, 0, 0, tiled=True)
    their_rows = lax.ppermute(wanted, HEAD, [(i, i ^ 1) for i in range(split)])
    rows, whole = pl.pallas_call(
        copies_kernel,
        out_shape=(
            jax.ShapeDtypeStruct((others, 2, features // 2), bf16),
            jax.ShapeDtypeStruct((docs, features), f32),
        ),
        in_specs=[VMEM],
        out_specs=(VMEM, VMEM),
        compiler_params=small,
        name="copies",
    )(got)
    every = lax.all_to_all(rows, line, 0, 0, axis_index_groups=groups, tiled=True)
    every = every.reshape(lanes, features // 2)
    pos = positives.reshape(others, cores * split)
    pair = lax.all_gather(whole, DP[3])

    stats, logits, chosen, unit, rnorm = pl.pallas_call(
        logits_kernel,
        out_shape=(
            jax.ShapeDtypeStruct((others, 2, lanes), f32),
            jax.ShapeDtypeStruct((cores * docs, lanes), f32),
            jax.ShapeDtypeStruct((cores * docs, lanes), f32),
            jax.ShapeDtypeStruct((cores * docs, features), f32),
            jax.ShapeDtypeStruct((cores * docs, HD), f32),
        ),
        in_specs=[VMEM] * 3,
        out_specs=(VMEM,) * 5,
        compiler_params=small,
        name="logits",
    )(pair, every, pos)
    stats = lax.all_to_all(stats, line, 0, 0, axis_index_groups=groups, tiled=True)

    grads = pl.pallas_call(
        slopes_kernel,
        out_shape=jax.ShapeDtypeStruct((cores * split, docs, features + lanes), bf16),
        in_specs=[VMEM] * 6,
        out_specs=VMEM,
        compiler_params=small,
        name="slopes",
    )(stats, logits, chosen, unit, rnorm, every)
    grads = lax.all_to_all(grads, (DP[3], *HEAD), 0, 0, tiled=True)

    d_values, loss = pl.pallas_call(
        values_kernel,
        out_shape=(
            jax.ShapeDtypeStruct((half, seq_len), bf16),
            jax.ShapeDtypeStruct((1, 1), f32),
        ),
        in_specs=[SMEM] + [VMEM] * 4,
        out_specs=(VMEM, VMEM),
        compiler_params=small,
        name="slopes_of_values",
    )(lengths, grads, out_weight, their_rows, got)
    return d_values.T, loss.reshape(())


def solution(mesh):
    shape = (4, 8, 2, 2) if mesh.devices.size == 512 else (1, mesh.devices.size // 16, 2, 2)
    head = mesh.shape["head"]
    torus = Mesh(mesh.devices.reshape(*shape, head // 2, 2), (*DP, *HEAD))
    placed = (
        P(DP, HEAD),
        P(DP, None),
        P(DP, None),
        P(HEAD, None),
        P(DP, None),
        P(DP, HEAD),
        P(),
    )
    return jax.shard_map(
        per_device, mesh=torus, in_specs=placed, out_specs=(P(DP, HEAD), P()), check_vma=False
    )
```

```python
import math

import jax
import jax.numpy as jnp
from jax import lax
from jax.experimental import pallas as pl
from jax.experimental.pallas import tpu as pltpu
from jax.sharding import Mesh
from jax.sharding import PartitionSpec as P

HEADS = 12
KV_HEADS = 2
HD = 128
DP = ("dp_0", "dp_1", "dp_2", "dp_3")
LONGEST = 256
HEAD = ("head_0", "head_1")

sim_scale = 20.0
loss_scale = 32768.0

NT = (((1,), (1,)), ((), ()))
TN = (((0,), (0,)), ((), ()))
VMEM = pl.BlockSpec(memory_space=pltpu.VMEM)
HBM = pl.BlockSpec(memory_space=pl.ANY)
SMEM = pl.BlockSpec(memory_space=pltpu.SMEM)


def query_class():
    return lax.axis_index(HEAD) ^ (2 * lax.axis_index(DP[2]))


def class_groups():
    split, uppers = lax.axis_size(HEAD), lax.axis_size(DP[2])
    blocks = lax.axis_size(DP[:2])
    return [
        [(b * uppers + u) * split + (k ^ (2 * u)) for b in range(blocks) for u in range(uppers)]
        for k in range(split)
    ]


def three_terms(value):
    high = value.astype(jnp.bfloat16)
    rest = value - high.astype(jnp.float32)
    mid = rest.astype(jnp.bfloat16)
    low = (rest - mid.astype(jnp.float32)).astype(jnp.bfloat16)
    return jnp.concatenate([high, mid, low], axis=0)


def of_three(value):
    rows = value.shape[0] // 3
    return value[:rows] + value[rows : 2 * rows] + value[2 * rows :]


def exact_dot(value, other, dims):
    return of_three(
        lax.dot_general(three_terms(value), other, dims, preferred_element_type=jnp.float32)
    )


def document_of(lens_ref, docs, shape, dim):
    place = lax.broadcasted_iota(jnp.int32, shape, dim)
    seg = jnp.zeros(shape, jnp.int32)
    start = jnp.zeros(shape, jnp.int32)
    end = jnp.int32(0)
    for j in range(docs):
        end = end + lens_ref[0, j]
        past = place >= end
        seg = seg + past.astype(jnp.int32)
        start = jnp.where(past, end, start)
    return seg, start


def lens_column(lens_ref, docs):
    row = lax.broadcasted_iota(jnp.int32, (docs, 1), 0)
    column = jnp.zeros((docs, 1), jnp.int32)
    for j in range(docs):
        column = jnp.where(row == j, lens_ref[0, j], column)
    return column.astype(jnp.float32)


def attend_kernel(
    lens_ref, q_hbm, k_hbm, v_hbm, w_hbm, queries_ref, sent_ref, rows_ref,
    q_ref, k_ref, v_ref, w_ref, total, done,
):
    copies = [
        pltpu.make_async_copy(source, target, done.at[i])
        for i, (source, target) in enumerate(
            ((q_hbm, q_ref), (k_hbm, k_ref), (v_hbm, v_ref), (w_hbm, w_ref))
        )
    ]
    for copy in copies:
        copy.start()
    seq_len, width = q_ref.shape
    heads = width // HD
    docs = lens_ref.shape[1]
    kv_head = lax.axis_index(HEAD) * heads // (HEADS // KV_HEADS)
    columns = pl.ds(pl.multiple_of(kv_head * HD, HD), HD)
    seg, start = document_of(lens_ref, docs, (1, seq_len), 1)
    total[...] = jnp.zeros_like(total)
    block = min(128, seq_len)
    factor = math.log2(math.e) / math.sqrt(HD)
    lane = lax.broadcasted_iota(jnp.int32, (heads * block, HD), 1)
    head = lax.broadcasted_iota(jnp.int32, (heads * block, HD), 0) // block
    pick = (lane == head).astype(jnp.bfloat16)
    copies[0].wait()
    copies[1].wait()
    for first in range(0, seq_len, block):
        low = max(0, (first - LONGEST + 1) // block * block)
        span = first + block - low
        k_block = k_ref[low : first + block, columns]
        k_place = low + lax.broadcasted_iota(jnp.int32, (span, block), 0)
        q_place = first + lax.broadcasted_iota(jnp.int32, (span, block), 1)
        allowed = (k_place <= q_place) & (k_place >= start[:, first : first + block])
        q_block = jnp.concatenate(
            [q_ref[first : first + block, h * HD : (h + 1) * HD] for h in range(heads)], axis=0
        )
        scores = lax.dot_general(k_block, q_block, NT, preferred_element_type=jnp.float32)
        probs = []
        for h in range(heads):
            mine = jnp.where(allowed, scores[:, h * block : (h + 1) * block], -1e30)
            top = jnp.max(mine, axis=0, keepdims=True)
            expo = jnp.exp2((mine - top) * factor)
            norm = 1.0 / jnp.sum(expo, axis=0, keepdims=True)
            probs.append((expo * norm).astype(jnp.bfloat16))
        total[low : first + block, :] += jnp.dot(
            jnp.concatenate(probs, axis=1), pick, preferred_element_type=jnp.float32
        )
    by_head = total[...].T
    member = lax.broadcasted_iota(jnp.int32, (docs, seq_len), 0) == seg
    shares = jnp.concatenate(
        [jnp.where(member, by_head[h : h + 1, :], 0.0) for h in range(heads)], axis=0
    )
    copies[2].wait()
    sums = exact_dot(shares, v_ref[:, columns], (((1,), (0,)), ((), ())))
    pooled = jnp.concatenate(
        [sums[h * docs : (h + 1) * docs] for h in range(heads)], axis=1
    ) / lens_column(lens_ref, docs)
    copies[3].wait()
    emb = exact_dot(pooled, w_ref[...], (((1,), (0,)), ((), ())))
    features = emb.shape[1]
    queries = queries_ref[...].astype(jnp.float32)
    place = lax.broadcasted_iota(jnp.int32, queries.shape, 0)
    middle = seq_len // 2
    pad = jnp.zeros((1, 2 * middle - width), jnp.float32)
    for k in range(sent_ref.shape[0]):
        row = jnp.where(place == k ^ (2 * lax.axis_index(DP[2])), queries, 0.0)
        row = jnp.sum(row, axis=0, keepdims=True)
        sent_ref[k, :, :features] = emb
        sent_ref[k, :, features:] = jnp.concatenate(
            [
                by_head[:heads, :middle],
                by_head[:heads, middle:],
                row[:, :middle],
                jnp.concatenate([row[:, middle:], pad], axis=1),
            ],
            axis=0,
        )
    half = HD // 2
    for h in range(heads):
        wanted = pl.ds(pl.multiple_of(h * HD + (1 - lax.axis_index(HEAD[1])) * half, half), half)
        rows_ref[h * half : (h + 1) * half, :] = w_ref[wanted, :]


def copies_kernel(got_ref, out_ref, whole_ref):
    docs, features = whole_ref.shape
    split = got_ref.shape[0]
    width = features // split
    place = 2 * (HEADS // split)
    parts = []
    for k in range(split):
        line = got_ref[k, place:, features:]
        middle = line.shape[1]
        parts += [line[:1, :], line[1:, : width - middle]]
    middle = split
    halves = [jnp.concatenate(parts[:middle], axis=1), jnp.concatenate(parts[middle:], axis=1)]
    both = jnp.concatenate(halves, axis=0).astype(jnp.bfloat16)
    out_ref[...] = jnp.broadcast_to(both[None], out_ref.shape)
    whole = got_ref[0, :, :features]
    for k in range(1, split):
        whole = whole + got_ref[k, :, :features]
    whole_ref[...] = whole


def pair_logits(unit, q_ref):
    half = q_ref.shape[1]
    docs = unit.shape[0]
    both = jnp.concatenate([unit[:, :half], unit[:, half:]], axis=0)
    parts = lax.dot_general(both, q_ref[...], NT, preferred_element_type=jnp.float32)
    even = lax.broadcasted_iota(jnp.int32, (docs, q_ref.shape[0]), 1) % 2 == 0
    mine = jnp.where(even, parts[:docs], parts[docs:])
    width = mine.shape[1]
    other = jnp.where(even, pltpu.roll(mine, width - 1, 1), pltpu.roll(mine, 1, 1))
    return sim_scale * (mine + other)


def positive_mask(pos_ref, docs):
    count, classes = pos_ref.shape
    mine = lax.broadcasted_iota(jnp.int32, (count, classes), 1) == (
        lax.axis_size(HEAD) * lax.axis_index(DP[3]) + query_class()
    )
    lane = lax.broadcasted_iota(jnp.int32, (count, 2 * count), 1)
    row = lax.broadcasted_iota(jnp.int32, (count, 2 * count), 0)
    spread = (lane // 2 == row).astype(jnp.bfloat16)
    pos = jnp.where(mine, pos_ref[...], 0)

    def spread_out(digit):
        lines = lax.dot_general(
            digit.astype(jnp.float32).astype(jnp.bfloat16), spread, TN,
            preferred_element_type=jnp.float32,
        )
        return jnp.sum(lines, axis=0, keepdims=True)

    positive = 128.0 * spread_out(pos // 128) + spread_out(pos % 128)
    me = lax.axis_index(DP[:3])
    row = lax.broadcasted_iota(jnp.int32, (docs, 2 * count), 0)
    owned = jnp.concatenate([me * docs + row, (me ^ 1) * docs + row], axis=0)
    return (positive == owned.astype(jnp.float32)).astype(jnp.float32)


def logits_kernel(
    emb_ref, other_ref, q_ref, pos_ref, out_ref, logits_ref, chosen_ref, unit_ref, rnorm_ref
):
    docs = logits_ref.shape[0]
    emb = [ref[k] for ref in (emb_ref, other_ref) for k in range(ref.shape[0])]
    emb = jnp.concatenate(emb, axis=0)
    rnorm = 1.0 / jnp.sqrt(jnp.sum(emb * emb, axis=1, keepdims=True) + 1e-06)
    unit = emb * rnorm
    logits = pair_logits(unit.astype(jnp.bfloat16), q_ref)
    chosen = positive_mask(pos_ref, docs)
    top = jnp.max(logits, axis=0, keepdims=True)
    expo = jnp.exp(logits - top)
    total = jnp.sum(expo[:docs], axis=0, keepdims=True) + jnp.sum(expo[docs:], axis=0, keepdims=True)
    lse = top + jnp.log(total)
    hits = logits * chosen
    positive = jnp.sum(hits[:docs], axis=0, keepdims=True) + jnp.sum(
        hits[docs:], axis=0, keepdims=True
    )
    out_ref[...] = jnp.broadcast_to(
        jnp.concatenate([lse, positive], axis=0)[None], out_ref.shape
    )
    logits_ref[...] = logits[:docs]
    chosen_ref[...] = chosen[:docs]
    unit_ref[...] = unit[:docs]
    rnorm_ref[...] = jnp.broadcast_to(rnorm[:docs], rnorm_ref.shape)


def slopes_kernel(stats_ref, logits_ref, chosen_ref, unit_ref, rnorm_ref, q_ref, out_ref):
    pair_docs = logits_ref.shape[0]
    half = q_ref.shape[1]
    features = 2 * half
    split = out_ref.shape[0] // 2
    docs = pair_docs // 2
    each = stats_ref[:, 0, :]
    top = jnp.max(each, axis=0, keepdims=True)
    lse = top + jnp.log(jnp.sum(jnp.exp(each - top), axis=0, keepdims=True))
    positive = jnp.sum(stats_ref[:, 1, :], axis=0, keepdims=True)
    slopes = jnp.exp(logits_ref[...] - lse) - chosen_ref[...]
    even = lax.broadcasted_iota(jnp.int32, slopes.shape, 1) % 2 == 0
    both = jnp.concatenate([jnp.where(even, slopes, 0.0), jnp.where(even, 0.0, slopes)], axis=0)
    parts = sim_scale * exact_dot(both, q_ref[...], (((1,), (0,)), ((), ())))
    grads = jnp.concatenate([parts[:pair_docs], parts[pair_docs:]], axis=1)
    unit = unit_ref[...]
    inner = jnp.sum(unit * grads, axis=1, keepdims=True)
    grads = (rnorm_ref[:, :1] * (grads - unit * inner)).astype(jnp.bfloat16)
    losses = jnp.broadcast_to(lse - positive, (docs, lse.shape[1]))
    row = lax.broadcasted_iota(jnp.int32, losses.shape, 0)
    high = losses.astype(jnp.bfloat16).astype(jnp.float32)
    mid = (losses - high).astype(jnp.bfloat16).astype(jnp.float32)
    losses = jnp.where(row == 0, high, jnp.where(row == 1, mid, losses - high - mid))
    for k in range(2 * split):
        core = k // split
        out_ref[k, :, :features] = grads[core * docs : (core + 1) * docs]
        out_ref[k, :, features:] = losses.astype(jnp.bfloat16)


def values_kernel(lens_ref, grads_ref, my_rows_ref, their_rows_ref, got_ref, out_ref, loss_ref):
    docs = lens_ref.shape[1]
    features = my_rows_ref.shape[1]
    seq_len = out_ref.shape[1]
    half = HD // 2
    heads = my_rows_ref.shape[0] // HD
    low = lax.axis_index(HEAD[1])
    grads = grads_ref[0].astype(jnp.float32)
    for k in range(1, grads_ref.shape[0]):
        grads = grads + grads_ref[k].astype(jnp.float32)
    lanes = grads.shape[1] - features
    loss_ref[...] = jnp.sum(
        jnp.sum(grads[:3, features:], axis=0, keepdims=True), axis=1, keepdims=True
    ) / (grads_ref.shape[0] * lanes)
    rows = [
        my_rows_ref[pl.ds(pl.multiple_of(h * HD + low * half, half), half), :]
        for h in range(heads)
    ]
    rows = jnp.concatenate([*rows, their_rows_ref[...]], axis=0)
    terms = three_terms(grads[:, :features])
    slopes = lax.dot_general(rows, terms, NT, preferred_element_type=jnp.float32)
    slopes = slopes[:, :docs] + slopes[:, docs : 2 * docs] + slopes[:, 2 * docs :]
    lane = lax.broadcasted_iota(jnp.int32, (1, docs), 1)
    lens = jnp.zeros((1, docs), jnp.int32)
    for j in range(docs):
        lens = jnp.where(lane == j, lens_ref[0, j], lens)
    slopes = (slopes / lens.astype(jnp.float32) * loss_scale).astype(jnp.bfloat16)
    slopes = [slopes[h * half : (h + 1) * half] for h in range(2 * heads)]
    seg, _ = document_of(lens_ref, docs, (1, seq_len), 1)
    member = lax.broadcasted_iota(jnp.int32, (docs, seq_len), 0) == seg
    me = lax.axis_index(HEAD)
    shares = []
    for owner in (me, me ^ 1):
        sums = got_ref[owner, :, features:]
        sums = jnp.concatenate([sums[:heads], sums[heads : 2 * heads]], axis=1)
        shares += [jnp.where(member, sums[h : h + 1], 0.0) for h in range(heads)]
    out = jnp.dot(
        jnp.concatenate(slopes * 3, axis=1),
        three_terms(jnp.concatenate(shares, axis=0)),
        preferred_element_type=jnp.float32,
    )
    out_ref[...] = out.astype(jnp.bfloat16)


def per_device(attn_queries, keys, values, out_weight, lengths, queries, positives):
    seq_len, width = attn_queries.shape
    heads = width // HD
    docs = lengths.shape[1]
    features = out_weight.shape[1]
    split = lax.axis_size(HEAD)
    cores = lax.axis_size(DP[3])
    others = lax.axis_size(DP[:3])
    lanes = 2 * others
    f32, bf16 = jnp.float32, jnp.bfloat16
    big = pltpu.CompilerParams(vmem_limit_bytes=60 * 2**20)
    small = pltpu.CompilerParams(vmem_limit_bytes=16 * 2**20)

    half = HD // 2
    line = (*DP[:3], *HEAD)
    groups = class_groups()

    partial, wanted = pl.pallas_call(
        attend_kernel,
        out_shape=(
            jax.ShapeDtypeStruct((split, docs, features + seq_len // 2), f32),
            jax.ShapeDtypeStruct((heads * half, features), bf16),
        ),
        in_specs=[SMEM] + [HBM] * 4 + [VMEM],
        out_specs=(VMEM, VMEM),
        scratch_shapes=[
            *(pltpu.VMEM(a.shape, a.dtype) for a in (attn_queries, keys, values, out_weight)),
            pltpu.VMEM((seq_len, HD), f32),
            pltpu.SemaphoreType.DMA((4,)),
        ],
        compiler_params=big,
        name="attend",
    )(lengths, attn_queries, keys, values, out_weight, queries)
    got = lax.all_to_all(partial, HEAD, 0, 0, tiled=True)
    their_rows = lax.ppermute(wanted, HEAD, [(i, i ^ 1) for i in range(split)])
    rows, whole = pl.pallas_call(
        copies_kernel,
        out_shape=(
            jax.ShapeDtypeStruct((others, 2, features // 2), bf16),
            jax.ShapeDtypeStruct((docs, features), f32),
        ),
        in_specs=[VMEM],
        out_specs=(VMEM, VMEM),
        compiler_params=small,
        name="copies",
    )(got)
    every = lax.all_to_all(rows, line, 0, 0, axis_index_groups=groups, tiled=True)
    every = every.reshape(lanes, features // 2)
    pos = positives.reshape(others, cores * split)
    whole, their_rows = lax.optimization_barrier((whole, their_rows))
    uppers = lax.axis_size(DP[2])
    across = [(i, i ^ (split + 2)) for i in range(uppers * split)]
    other = lax.ppermute(whole, (DP[2], *HEAD), across)
    pair = lax.all_gather(whole, DP[3])
    other = lax.all_gather(other, DP[3])

    stats, logits, chosen, unit, rnorm = pl.pallas_call(
        logits_kernel,
        out_shape=(
            jax.ShapeDtypeStruct((others // uppers, 2, lanes), f32),
            jax.ShapeDtypeStruct((cores * docs, lanes), f32),
            jax.ShapeDtypeStruct((cores * docs, lanes), f32),
            jax.ShapeDtypeStruct((cores * docs, features), f32),
            jax.ShapeDtypeStruct((cores * docs, HD), f32),
        ),
        in_specs=[VMEM] * 4,
        out_specs=(VMEM,) * 5,
        compiler_params=small,
        name="logits",
    )(pair, other, every, pos)
    stats = lax.all_to_all(stats, DP[:2], 0, 0, tiled=True)

    grads = pl.pallas_call(
        slopes_kernel,
        out_shape=jax.ShapeDtypeStruct((cores * split, docs, features + lanes), bf16),
        in_specs=[VMEM] * 6,
        out_specs=VMEM,
        compiler_params=small,
        name="slopes",
    )(stats, logits, chosen, unit, rnorm, every)
    grads = lax.all_to_all(grads, (DP[3], *HEAD), 0, 0, tiled=True)

    d_values, loss = pl.pallas_call(
        values_kernel,
        out_shape=(
            jax.ShapeDtypeStruct((half, seq_len), bf16),
            jax.ShapeDtypeStruct((1, 1), f32),
        ),
        in_specs=[SMEM] + [VMEM] * 4,
        out_specs=(VMEM, VMEM),
        compiler_params=small,
        name="slopes_of_values",
    )(lengths, grads, out_weight, their_rows, got)
    return d_values.T, loss.reshape(())


def solution(mesh):
    shape = (4, 8, 2, 2) if mesh.devices.size == 512 else (1, mesh.devices.size // 16, 2, 2)
    head = mesh.shape["head"]
    torus = Mesh(mesh.devices.reshape(*shape, head // 2, 2), (*DP, *HEAD))
    placed = (
        P(DP, HEAD),
        P(DP, None),
        P(DP, None),
        P(HEAD, None),
        P(DP, None),
        P(DP, HEAD),
        P(),
    )
    return jax.shard_map(
        per_device, mesh=torus, in_specs=placed, out_specs=(P(DP, HEAD), P()), check_vma=False
    )
```

```python
import math

import jax
import jax.numpy as jnp
from jax import lax
from jax.experimental import pallas as pl
from jax.experimental.pallas import tpu as pltpu
from jax.sharding import Mesh
from jax.sharding import PartitionSpec as P

HEADS = 12
KV_HEADS = 2
HD = 128
DP = ("dp_0", "dp_1", "dp_2", "dp_3")
LONGEST = 256
HEAD = ("head_0", "head_1")

sim_scale = 20.0
loss_scale = 32768.0

NT = (((1,), (1,)), ((), ()))
TN = (((0,), (0,)), ((), ()))
VMEM = pl.BlockSpec(memory_space=pltpu.VMEM)
SMEM = pl.BlockSpec(memory_space=pltpu.SMEM)


def query_class():
    return lax.axis_index(HEAD) ^ (2 * lax.axis_index(DP[2]))


def class_groups():
    split, uppers = lax.axis_size(HEAD), lax.axis_size(DP[2])
    blocks = lax.axis_size(DP[:2])
    return [
        [(b * uppers + u) * split + (k ^ (2 * u)) for b in range(blocks) for u in range(uppers)]
        for k in range(split)
    ]


def three_terms(value):
    high = value.astype(jnp.bfloat16)
    rest = value - high.astype(jnp.float32)
    mid = rest.astype(jnp.bfloat16)
    low = (rest - mid.astype(jnp.float32)).astype(jnp.bfloat16)
    return jnp.concatenate([high, mid, low], axis=0)


def of_three(value):
    rows = value.shape[0] // 3
    return value[:rows] + value[rows : 2 * rows] + value[2 * rows :]


def exact_dot(value, other, dims):
    return of_three(
        lax.dot_general(three_terms(value), other, dims, preferred_element_type=jnp.float32)
    )


def document_of(lens_ref, docs, shape, dim):
    place = lax.broadcasted_iota(jnp.int32, shape, dim)
    seg = jnp.zeros(shape, jnp.int32)
    start = jnp.zeros(shape, jnp.int32)
    end = jnp.int32(0)
    for j in range(docs):
        end = end + lens_ref[0, j]
        past = place >= end
        seg = seg + past.astype(jnp.int32)
        start = jnp.where(past, end, start)
    return seg, start


def lens_column(lens_ref, docs):
    row = lax.broadcasted_iota(jnp.int32, (docs, 1), 0)
    column = jnp.zeros((docs, 1), jnp.int32)
    for j in range(docs):
        column = jnp.where(row == j, lens_ref[0, j], column)
    return column.astype(jnp.float32)


def attend_kernel(
    lens_ref, q_ref, k_ref, v_ref, w_ref, queries_ref, sent_ref, rows_ref, total
):
    seq_len, width = q_ref.shape
    heads = width // HD
    docs = lens_ref.shape[1]
    kv_head = lax.axis_index(HEAD) * heads // (HEADS // KV_HEADS)
    columns = pl.ds(pl.multiple_of(kv_head * HD, HD), HD)
    seg, start = document_of(lens_ref, docs, (1, seq_len), 1)
    total[...] = jnp.zeros_like(total)
    block = min(128, seq_len)
    factor = math.log2(math.e) / math.sqrt(HD)
    lane = lax.broadcasted_iota(jnp.int32, (block, HD), 1)
    for first in range(0, seq_len, block):
        low = max(0, (first - LONGEST + 1) // block * block)
        span = first + block - low
        k_block = k_ref[low : first + block, columns]
        k_place = low + lax.broadcasted_iota(jnp.int32, (span, block), 0)
        q_place = first + lax.broadcasted_iota(jnp.int32, (span, block), 1)
        allowed = (k_place <= q_place) & (k_place >= start[:, first : first + block])
        for h in range(heads):
            q_block = q_ref[first : first + block, h * HD : (h + 1) * HD]
            scores = lax.dot_general(k_block, q_block, NT, preferred_element_type=jnp.float32)
            scores = jnp.where(allowed, scores, -1e30)
            top = jnp.max(scores, axis=0, keepdims=True)
            expo = jnp.exp2((scores - top) * factor)
            norm = 1.0 / jnp.sum(expo, axis=0, keepdims=True)
            probs = (expo * norm).astype(jnp.bfloat16)
            pick = (lane == h).astype(jnp.bfloat16)
            total[low : first + block, :] += jnp.dot(
                probs, pick, preferred_element_type=jnp.float32
            )
    by_head = total[...].T
    member = lax.broadcasted_iota(jnp.int32, (docs, seq_len), 0) == seg
    shares = jnp.concatenate(
        [jnp.where(member, by_head[h : h + 1, :], 0.0) for h in range(heads)], axis=0
    )
    sums = exact_dot(shares, v_ref[:, columns], (((1,), (0,)), ((), ())))
    pooled = jnp.concatenate(
        [sums[h * docs : (h + 1) * docs] for h in range(heads)], axis=1
    ) / lens_column(lens_ref, docs)
    emb = exact_dot(pooled, w_ref[...], (((1,), (0,)), ((), ())))
    features = emb.shape[1]
    queries = queries_ref[...].astype(jnp.float32)
    place = lax.broadcasted_iota(jnp.int32, queries.shape, 0)
    middle = seq_len // 2
    pad = jnp.zeros((1, 2 * middle - width), jnp.float32)
    for k in range(sent_ref.shape[0]):
        row = jnp.where(place == k ^ (2 * lax.axis_index(DP[2])), queries, 0.0)
        row = jnp.sum(row, axis=0, keepdims=True)
        sent_ref[k, :, :features] = emb
        sent_ref[k, :, features:] = jnp.concatenate(
            [
                by_head[:heads, :middle],
                by_head[:heads, middle:],
                row[:, :middle],
                jnp.concatenate([row[:, middle:], pad], axis=1),
            ],
            axis=0,
        )
    half = HD // 2
    for h in range(heads):
        place = pl.multiple_of(h * HD + (1 - lax.axis_index(HEAD[1])) * half, half)
        rows_ref[h * half : (h + 1) * half, :] = w_ref[pl.ds(place, half), :]


def copies_kernel(got_ref, out_ref, whole_ref):
    docs, features = whole_ref.shape
    split = got_ref.shape[0]
    width = features // split
    place = 2 * (HEADS // split)
    parts = []
    for k in range(split):
        line = got_ref[k, place:, features:]
        middle = line.shape[1]
        parts += [line[:1, :], line[1:, : width - middle]]
    middle = split
    halves = [jnp.concatenate(parts[:middle], axis=1), jnp.concatenate(parts[middle:], axis=1)]
    both = jnp.concatenate(halves, axis=0).astype(jnp.bfloat16)
    out_ref[...] = jnp.broadcast_to(both[None], out_ref.shape)
    whole = got_ref[0, :, :features]
    for k in range(1, split):
        whole = whole + got_ref[k, :, :features]
    whole_ref[...] = whole


def pair_logits(unit, q_ref):
    half = q_ref.shape[1]
    docs = unit.shape[0]
    both = jnp.concatenate([unit[:, :half], unit[:, half:]], axis=0)
    parts = lax.dot_general(both, q_ref[...], NT, preferred_element_type=jnp.float32)
    even = lax.broadcasted_iota(jnp.int32, (docs, q_ref.shape[0]), 1) % 2 == 0
    mine = jnp.where(even, parts[:docs], parts[docs:])
    width = mine.shape[1]
    other = jnp.where(even, pltpu.roll(mine, width - 1, 1), pltpu.roll(mine, 1, 1))
    return sim_scale * (mine + other)


def positive_mask(pos_ref, docs):
    count, classes = pos_ref.shape
    mine = lax.broadcasted_iota(jnp.int32, (count, classes), 1) == (
        lax.axis_size(HEAD) * lax.axis_index(DP[3]) + query_class()
    )
    lane = lax.broadcasted_iota(jnp.int32, (count, 2 * count), 1)
    row = lax.broadcasted_iota(jnp.int32, (count, 2 * count), 0)
    spread = (lane // 2 == row).astype(jnp.bfloat16)
    pos = jnp.where(mine, pos_ref[...], 0)

    def spread_out(digit):
        lines = lax.dot_general(
            digit.astype(jnp.float32).astype(jnp.bfloat16), spread, TN,
            preferred_element_type=jnp.float32,
        )
        return jnp.sum(lines, axis=0, keepdims=True)

    positive = 128.0 * spread_out(pos // 128) + spread_out(pos % 128)
    me = lax.axis_index(DP[:3])
    row = lax.broadcasted_iota(jnp.int32, (docs, 2 * count), 0)
    owned = jnp.concatenate([me * docs + row, (me ^ 1) * docs + row], axis=0)
    return (positive == owned.astype(jnp.float32)).astype(jnp.float32)


def logits_kernel(
    emb_ref, q_ref, pos_ref, out_ref, logits_ref, chosen_ref, unit_ref, rnorm_ref
):
    docs = logits_ref.shape[0]
    me = lax.axis_index(DP[2])
    emb = [emb_ref[core, upper] for upper in (me, 1 - me) for core in range(emb_ref.shape[0])]
    emb = jnp.concatenate(emb, axis=0)
    rnorm = 1.0 / jnp.sqrt(jnp.sum(emb * emb, axis=1, keepdims=True) + 1e-06)
    unit = emb * rnorm
    logits = pair_logits(unit.astype(jnp.bfloat16), q_ref)
    chosen = positive_mask(pos_ref, docs)
    top = jnp.max(logits, axis=0, keepdims=True)
    expo = jnp.exp(logits - top)
    total = jnp.sum(expo[:docs], axis=0, keepdims=True) + jnp.sum(expo[docs:], axis=0, keepdims=True)
    lse = top + jnp.log(total)
    hits = logits * chosen
    positive = jnp.sum(hits[:docs], axis=0, keepdims=True) + jnp.sum(
        hits[docs:], axis=0, keepdims=True
    )
    out_ref[...] = jnp.broadcast_to(
        jnp.concatenate([lse, positive], axis=0)[None], out_ref.shape
    )
    logits_ref[...] = logits[:docs]
    chosen_ref[...] = chosen[:docs]
    unit_ref[...] = unit[:docs]
    rnorm_ref[...] = jnp.broadcast_to(rnorm[:docs], rnorm_ref.shape)


def slopes_kernel(stats_ref, logits_ref, chosen_ref, unit_ref, rnorm_ref, q_ref, out_ref):
    pair_docs = logits_ref.shape[0]
    half = q_ref.shape[1]
    features = 2 * half
    split = out_ref.shape[0] // 2
    docs = pair_docs // 2
    each = stats_ref[:, 0, :]
    top = jnp.max(each, axis=0, keepdims=True)
    lse = top + jnp.log(jnp.sum(jnp.exp(each - top), axis=0, keepdims=True))
    positive = jnp.sum(stats_ref[:, 1, :], axis=0, keepdims=True)
    slopes = jnp.exp(logits_ref[...] - lse) - chosen_ref[...]
    even = lax.broadcasted_iota(jnp.int32, slopes.shape, 1) % 2 == 0
    both = jnp.concatenate([jnp.where(even, slopes, 0.0), jnp.where(even, 0.0, slopes)], axis=0)
    parts = sim_scale * exact_dot(both, q_ref[...], (((1,), (0,)), ((), ())))
    grads = jnp.concatenate([parts[:pair_docs], parts[pair_docs:]], axis=1)
    unit = unit_ref[...]
    inner = jnp.sum(unit * grads, axis=1, keepdims=True)
    grads = (rnorm_ref[:, :1] * (grads - unit * inner)).astype(jnp.bfloat16)
    losses = jnp.broadcast_to(lse - positive, (docs, lse.shape[1]))
    row = lax.broadcasted_iota(jnp.int32, losses.shape, 0)
    high = losses.astype(jnp.bfloat16).astype(jnp.float32)
    mid = (losses - high).astype(jnp.bfloat16).astype(jnp.float32)
    losses = jnp.where(row == 0, high, jnp.where(row == 1, mid, losses - high - mid))
    for k in range(2 * split):
        core = k // split
        out_ref[k, :, :features] = grads[core * docs : (core + 1) * docs]
        out_ref[k, :, features:] = losses.astype(jnp.bfloat16)


def values_kernel(lens_ref, grads_ref, my_rows_ref, their_rows_ref, got_ref, out_ref, loss_ref):
    docs = lens_ref.shape[1]
    features = my_rows_ref.shape[1]
    seq_len = out_ref.shape[1]
    half = HD // 2
    heads = my_rows_ref.shape[0] // HD
    low = lax.axis_index(HEAD[1])
    grads = grads_ref[0].astype(jnp.float32)
    for k in range(1, grads_ref.shape[0]):
        grads = grads + grads_ref[k].astype(jnp.float32)
    lanes = grads.shape[1] - features
    loss_ref[...] = jnp.sum(
        jnp.sum(grads[:3, features:], axis=0, keepdims=True), axis=1, keepdims=True
    ) / (grads_ref.shape[0] * lanes)
    rows = [
        my_rows_ref[pl.ds(pl.multiple_of(h * HD + low * half, half), half), :]
        for h in range(heads)
    ]
    rows = jnp.concatenate([*rows, their_rows_ref[...]], axis=0)
    terms = three_terms(grads[:, :features])
    slopes = lax.dot_general(rows, terms, NT, preferred_element_type=jnp.float32)
    slopes = slopes[:, :docs] + slopes[:, docs : 2 * docs] + slopes[:, 2 * docs :]
    lane = lax.broadcasted_iota(jnp.int32, (1, docs), 1)
    lens = jnp.zeros((1, docs), jnp.int32)
    for j in range(docs):
        lens = jnp.where(lane == j, lens_ref[0, j], lens)
    slopes = (slopes / lens.astype(jnp.float32) * loss_scale).astype(jnp.bfloat16)
    slopes = [slopes[h * half : (h + 1) * half] for h in range(2 * heads)]
    seg, _ = document_of(lens_ref, docs, (1, seq_len), 1)
    member = lax.broadcasted_iota(jnp.int32, (docs, seq_len), 0) == seg
    me = lax.axis_index(HEAD)
    shares = []
    for owner in (me, me ^ 1):
        sums = got_ref[owner, :, features:]
        sums = jnp.concatenate([sums[:heads], sums[heads : 2 * heads]], axis=1)
        shares += [jnp.where(member, sums[h : h + 1], 0.0) for h in range(heads)]
    out = jnp.dot(
        jnp.concatenate(slopes * 3, axis=1),
        three_terms(jnp.concatenate(shares, axis=0)),
        preferred_element_type=jnp.float32,
    )
    out_ref[...] = out.astype(jnp.bfloat16)


def per_device(attn_queries, keys, values, out_weight, lengths, queries, positives):
    seq_len, width = attn_queries.shape
    heads = width // HD
    docs = lengths.shape[1]
    features = out_weight.shape[1]
    split = lax.axis_size(HEAD)
    cores = lax.axis_size(DP[3])
    others = lax.axis_size(DP[:3])
    lanes = 2 * others
    f32, bf16 = jnp.float32, jnp.bfloat16
    big = pltpu.CompilerParams(vmem_limit_bytes=60 * 2**20)
    small = pltpu.CompilerParams(vmem_limit_bytes=16 * 2**20)

    half = HD // 2
    line = (*DP[:3], *HEAD)
    groups = class_groups()

    partial, wanted = pl.pallas_call(
        attend_kernel,
        out_shape=(
            jax.ShapeDtypeStruct((split, docs, features + seq_len // 2), f32),
            jax.ShapeDtypeStruct((heads * half, features), bf16),
        ),
        in_specs=[SMEM] + [VMEM] * 5,
        out_specs=(VMEM, VMEM),
        scratch_shapes=[pltpu.VMEM((seq_len, HD), f32)],
        compiler_params=big,
        name="attend",
    )(lengths, attn_queries, keys, values, out_weight, queries)
    got = lax.all_to_all(partial, HEAD, 0, 0, tiled=True)
    their_rows = lax.ppermute(wanted, HEAD, [(i, i ^ 1) for i in range(split)])
    rows, whole = pl.pallas_call(
        copies_kernel,
        out_shape=(
            jax.ShapeDtypeStruct((others, 2, features // 2), bf16),
            jax.ShapeDtypeStruct((docs, features), f32),
        ),
        in_specs=[VMEM],
        out_specs=(VMEM, VMEM),
        compiler_params=small,
        name="copies",
    )(got)
    every = lax.all_to_all(rows, line, 0, 0, axis_index_groups=groups, tiled=True)
    every = every.reshape(lanes, features // 2)
    pos = positives.reshape(others, cores * split)
    whole, their_rows = lax.optimization_barrier((whole, their_rows))
    uppers = lax.axis_size(DP[2])
    across = [[i, i ^ (split + 2)] for i in range(split)]
    whole = lax.all_gather(whole, (DP[2], *HEAD), axis_index_groups=across)
    whole = lax.all_gather(whole, DP[3])

    stats, logits, chosen, unit, rnorm = pl.pallas_call(
        logits_kernel,
        out_shape=(
            jax.ShapeDtypeStruct((others // uppers, 2, lanes), f32),
            jax.ShapeDtypeStruct((cores * docs, lanes), f32),
            jax.ShapeDtypeStruct((cores * docs, lanes), f32),
            jax.ShapeDtypeStruct((cores * docs, features), f32),
            jax.ShapeDtypeStruct((cores * docs, HD), f32),
        ),
        in_specs=[VMEM] * 3,
        out_specs=(VMEM,) * 5,
        compiler_params=small,
        name="logits",
    )(whole, every, pos)
    stats = lax.all_to_all(stats, DP[:2], 0, 0, tiled=True)

    grads = pl.pallas_call(
        slopes_kernel,
        out_shape=jax.ShapeDtypeStruct((cores * split, docs, features + lanes), bf16),
        in_specs=[VMEM] * 6,
        out_specs=VMEM,
        compiler_params=small,
        name="slopes",
    )(stats, logits, chosen, unit, rnorm, every)
    grads = lax.all_to_all(grads, (DP[3], *HEAD), 0, 0, tiled=True)

    d_values, loss = pl.pallas_call(
        values_kernel,
        out_shape=(
            jax.ShapeDtypeStruct((half, seq_len), bf16),
            jax.ShapeDtypeStruct((1, 1), f32),
        ),
        in_specs=[SMEM] + [VMEM] * 4,
        out_specs=(VMEM, VMEM),
        compiler_params=small,
        name="slopes_of_values",
    )(lengths, grads, out_weight, their_rows, got)
    return d_values.T, loss.reshape(())


def solution(mesh):
    shape = (4, 8, 2, 2) if mesh.devices.size == 512 else (1, mesh.devices.size // 16, 2, 2)
    head = mesh.shape["head"]
    torus = Mesh(mesh.devices.reshape(*shape, head // 2, 2), (*DP, *HEAD))
    placed = (
        P(DP, HEAD),
        P(DP, None),
        P(DP, None),
        P(HEAD, None),
        P(DP, None),
        P(DP, HEAD),
        P(),
    )
    return jax.shard_map(
        per_device, mesh=torus, in_specs=placed, out_specs=(P(DP, HEAD), P()), check_vma=False
    )
```

```python
import math

import jax
import jax.numpy as jnp
from jax import lax
from jax.experimental import pallas as pl
from jax.experimental.pallas import tpu as pltpu
from jax.sharding import Mesh
from jax.sharding import PartitionSpec as P

HEADS = 12
KV_HEADS = 2
HD = 128
DP = ("dp_0", "dp_1", "dp_2", "dp_3")
LONGEST = 256
HEAD = ("head_0", "head_1")

sim_scale = 20.0
loss_scale = 32768.0

NT = (((1,), (1,)), ((), ()))
TN = (((0,), (0,)), ((), ()))
VMEM = pl.BlockSpec(memory_space=pltpu.VMEM)
SMEM = pl.BlockSpec(memory_space=pltpu.SMEM)


def query_class():
    return lax.axis_index(HEAD) ^ (2 * lax.axis_index(DP[2]))


def class_groups():
    split, uppers = lax.axis_size(HEAD), lax.axis_size(DP[2])
    blocks = lax.axis_size(DP[:2])
    return [
        [(b * uppers + u) * split + (k ^ (2 * u)) for b in range(blocks) for u in range(uppers)]
        for k in range(split)
    ]


def three_terms(value):
    high = value.astype(jnp.bfloat16)
    rest = value - high.astype(jnp.float32)
    mid = rest.astype(jnp.bfloat16)
    low = (rest - mid.astype(jnp.float32)).astype(jnp.bfloat16)
    return jnp.concatenate([high, mid, low], axis=0)


def of_three(value):
    rows = value.shape[0] // 3
    return value[:rows] + value[rows : 2 * rows] + value[2 * rows :]


def exact_dot(value, other, dims):
    return of_three(
        lax.dot_general(three_terms(value), other, dims, preferred_element_type=jnp.float32)
    )


def document_of(lens_ref, docs, shape, dim):
    place = lax.broadcasted_iota(jnp.int32, shape, dim)
    seg = jnp.zeros(shape, jnp.int32)
    start = jnp.zeros(shape, jnp.int32)
    end = jnp.int32(0)
    for j in range(docs):
        end = end + lens_ref[0, j]
        past = place >= end
        seg = seg + past.astype(jnp.int32)
        start = jnp.where(past, end, start)
    return seg, start


def lens_column(lens_ref, docs):
    row = lax.broadcasted_iota(jnp.int32, (docs, 1), 0)
    column = jnp.zeros((docs, 1), jnp.int32)
    for j in range(docs):
        column = jnp.where(row == j, lens_ref[0, j], column)
    return column.astype(jnp.float32)


def attend_kernel(
    lens_ref, q_ref, k_ref, v_ref, w_ref, queries_ref, sent_ref, rows_ref, total
):
    seq_len, width = q_ref.shape
    heads = width // HD
    docs = lens_ref.shape[1]
    kv_head = lax.axis_index(HEAD) * heads // (HEADS // KV_HEADS)
    columns = pl.ds(pl.multiple_of(kv_head * HD, HD), HD)
    seg, start = document_of(lens_ref, docs, (1, seq_len), 1)
    total[...] = jnp.zeros_like(total)
    block = min(128, seq_len)
    factor = math.log2(math.e) / math.sqrt(HD)
    lane = lax.broadcasted_iota(jnp.int32, (block, HD), 1)
    for first in range(0, seq_len, block):
        low = max(0, (first - LONGEST + 1) // block * block)
        span = first + block - low
        k_block = k_ref[low : first + block, columns]
        k_place = low + lax.broadcasted_iota(jnp.int32, (span, block), 0)
        q_place = first + lax.broadcasted_iota(jnp.int32, (span, block), 1)
        allowed = (k_place <= q_place) & (k_place >= start[:, first : first + block])
        for h in range(heads):
            q_block = q_ref[first : first + block, h * HD : (h + 1) * HD]
            scores = lax.dot_general(k_block, q_block, NT, preferred_element_type=jnp.float32)
            scores = jnp.where(allowed, scores, -1e30)
            top = jnp.max(scores, axis=0, keepdims=True)
            expo = jnp.exp2((scores - top) * factor)
            norm = 1.0 / jnp.sum(expo, axis=0, keepdims=True)
            probs = (expo * norm).astype(jnp.bfloat16)
            pick = (lane == h).astype(jnp.bfloat16)
            total[low : first + block, :] += jnp.dot(
                probs, pick, preferred_element_type=jnp.float32
            )
    by_head = total[...].T
    member = lax.broadcasted_iota(jnp.int32, (docs, seq_len), 0) == seg
    shares = jnp.concatenate(
        [jnp.where(member, by_head[h : h + 1, :], 0.0) for h in range(heads)], axis=0
    )
    sums = exact_dot(shares, v_ref[:, columns], (((1,), (0,)), ((), ())))
    pooled = jnp.concatenate(
        [sums[h * docs : (h + 1) * docs] for h in range(heads)], axis=1
    ) / lens_column(lens_ref, docs)
    emb = exact_dot(pooled, w_ref[...], (((1,), (0,)), ((), ())))
    features = emb.shape[1]
    queries = queries_ref[...].astype(jnp.float32)
    place = lax.broadcasted_iota(jnp.int32, queries.shape, 0)
    middle = seq_len // 2
    pad = jnp.zeros((1, 2 * middle - width), jnp.float32)
    for k in range(sent_ref.shape[0]):
        row = jnp.where(place == k ^ (2 * lax.axis_index(DP[2])), queries, 0.0)
        row = jnp.sum(row, axis=0, keepdims=True)
        sent_ref[k, :, :features] = emb
        sent_ref[k, :, features:] = jnp.concatenate(
            [
                by_head[:heads, :middle],
                by_head[:heads, middle:],
                row[:, :middle],
                jnp.concatenate([row[:, middle:], pad], axis=1),
            ],
            axis=0,
        )
    half = HD // 2
    for h in range(heads):
        place = pl.multiple_of(h * HD + (1 - lax.axis_index(HEAD[1])) * half, half)
        rows_ref[h * half : (h + 1) * half, :] = w_ref[pl.ds(place, half), :]


def copies_kernel(got_ref, out_ref, whole_ref):
    docs, features = whole_ref.shape
    split = got_ref.shape[0]
    width = features // split
    place = 2 * (HEADS // split)
    parts = []
    for k in range(split):
        line = got_ref[k, place:, features:]
        middle = line.shape[1]
        parts += [line[:1, :], line[1:, : width - middle]]
    middle = split
    halves = [jnp.concatenate(parts[:middle], axis=1), jnp.concatenate(parts[middle:], axis=1)]
    both = jnp.concatenate(halves, axis=0).astype(jnp.bfloat16)
    out_ref[...] = jnp.broadcast_to(both[None], out_ref.shape)
    whole = got_ref[0, :, :features]
    for k in range(1, split):
        whole = whole + got_ref[k, :, :features]
    whole_ref[...] = whole


def pair_logits(unit, q_ref):
    half = q_ref.shape[1]
    docs = unit.shape[0]
    both = jnp.concatenate([unit[:, :half], unit[:, half:]], axis=0)
    parts = lax.dot_general(both, q_ref[...], NT, preferred_element_type=jnp.float32)
    even = lax.broadcasted_iota(jnp.int32, (docs, q_ref.shape[0]), 1) % 2 == 0
    mine = jnp.where(even, parts[:docs], parts[docs:])
    width = mine.shape[1]
    other = jnp.where(even, pltpu.roll(mine, width - 1, 1), pltpu.roll(mine, 1, 1))
    return sim_scale * (mine + other)


def positive_mask(pos_ref, docs):
    count, classes = pos_ref.shape
    mine = lax.broadcasted_iota(jnp.int32, (count, classes), 1) == (
        lax.axis_size(HEAD) * lax.axis_index(DP[3]) + query_class()
    )
    lane = lax.broadcasted_iota(jnp.int32, (count, 2 * count), 1)
    row = lax.broadcasted_iota(jnp.int32, (count, 2 * count), 0)
    spread = (lane // 2 == row).astype(jnp.bfloat16)
    pos = jnp.where(mine, pos_ref[...], 0)

    def spread_out(digit):
        lines = lax.dot_general(
            digit.astype(jnp.float32).astype(jnp.bfloat16), spread, TN,
            preferred_element_type=jnp.float32,
        )
        return jnp.sum(lines, axis=0, keepdims=True)

    positive = 128.0 * spread_out(pos // 128) + spread_out(pos % 128)
    me = lax.axis_index(DP[:3])
    row = lax.broadcasted_iota(jnp.int32, (docs, 2 * count), 0)
    owned = jnp.concatenate([me * docs + row, (me ^ 1) * docs + row], axis=0)
    return (positive == owned.astype(jnp.float32)).astype(jnp.float32)


def unit_kernel(emb_ref, unit_ref, rnorm_ref, rounded_ref):
    emb = jnp.concatenate([emb_ref[core] for core in range(emb_ref.shape[0])], axis=0)
    rnorm = 1.0 / jnp.sqrt(jnp.sum(emb * emb, axis=1, keepdims=True) + 1e-06)
    unit = emb * rnorm
    unit_ref[...] = unit
    rnorm_ref[...] = jnp.broadcast_to(rnorm, rnorm_ref.shape)
    rounded_ref[...] = unit.astype(jnp.bfloat16)


def logits_kernel(units_ref, q_ref, pos_ref, out_ref, logits_ref, chosen_ref):
    docs = logits_ref.shape[0]
    me = lax.axis_index(DP[2])
    logits = pair_logits(jnp.concatenate([units_ref[me], units_ref[1 - me]], axis=0), q_ref)
    chosen = positive_mask(pos_ref, docs)
    top = jnp.max(logits, axis=0, keepdims=True)
    expo = jnp.exp(logits - top)
    total = jnp.sum(expo[:docs], axis=0, keepdims=True) + jnp.sum(expo[docs:], axis=0, keepdims=True)
    lse = top + jnp.log(total)
    hits = logits * chosen
    positive = jnp.sum(hits[:docs], axis=0, keepdims=True) + jnp.sum(
        hits[docs:], axis=0, keepdims=True
    )
    out_ref[...] = jnp.broadcast_to(
        jnp.concatenate([lse, positive], axis=0)[None], out_ref.shape
    )
    logits_ref[...] = logits[:docs]
    chosen_ref[...] = chosen[:docs]


def slopes_kernel(stats_ref, logits_ref, chosen_ref, unit_ref, rnorm_ref, q_ref, out_ref):
    pair_docs = logits_ref.shape[0]
    half = q_ref.shape[1]
    features = 2 * half
    split = out_ref.shape[0] // 2
    docs = pair_docs // 2
    each = stats_ref[:, 0, :]
    top = jnp.max(each, axis=0, keepdims=True)
    lse = top + jnp.log(jnp.sum(jnp.exp(each - top), axis=0, keepdims=True))
    positive = jnp.sum(stats_ref[:, 1, :], axis=0, keepdims=True)
    slopes = jnp.exp(logits_ref[...] - lse) - chosen_ref[...]
    even = lax.broadcasted_iota(jnp.int32, slopes.shape, 1) % 2 == 0
    both = jnp.concatenate([jnp.where(even, slopes, 0.0), jnp.where(even, 0.0, slopes)], axis=0)
    parts = sim_scale * exact_dot(both, q_ref[...], (((1,), (0,)), ((), ())))
    grads = jnp.concatenate([parts[:pair_docs], parts[pair_docs:]], axis=1)
    unit = unit_ref[...]
    inner = jnp.sum(unit * grads, axis=1, keepdims=True)
    grads = (rnorm_ref[:, :1] * (grads - unit * inner)).astype(jnp.bfloat16)
    losses = jnp.broadcast_to(lse - positive, (docs, lse.shape[1]))
    row = lax.broadcasted_iota(jnp.int32, losses.shape, 0)
    high = losses.astype(jnp.bfloat16).astype(jnp.float32)
    mid = (losses - high).astype(jnp.bfloat16).astype(jnp.float32)
    losses = jnp.where(row == 0, high, jnp.where(row == 1, mid, losses - high - mid))
    for k in range(2 * split):
        core = k // split
        out_ref[k, :, :features] = grads[core * docs : (core + 1) * docs]
        out_ref[k, :, features:] = losses.astype(jnp.bfloat16)


def values_kernel(lens_ref, grads_ref, my_rows_ref, their_rows_ref, got_ref, out_ref, loss_ref):
    docs = lens_ref.shape[1]
    features = my_rows_ref.shape[1]
    seq_len = out_ref.shape[1]
    half = HD // 2
    heads = my_rows_ref.shape[0] // HD
    low = lax.axis_index(HEAD[1])
    grads = grads_ref[0].astype(jnp.float32)
    for k in range(1, grads_ref.shape[0]):
        grads = grads + grads_ref[k].astype(jnp.float32)
    lanes = grads.shape[1] - features
    loss_ref[...] = jnp.sum(
        jnp.sum(grads[:3, features:], axis=0, keepdims=True), axis=1, keepdims=True
    ) / (grads_ref.shape[0] * lanes)
    rows = [
        my_rows_ref[pl.ds(pl.multiple_of(h * HD + low * half, half), half), :]
        for h in range(heads)
    ]
    rows = jnp.concatenate([*rows, their_rows_ref[...]], axis=0)
    terms = three_terms(grads[:, :features])
    slopes = lax.dot_general(rows, terms, NT, preferred_element_type=jnp.float32)
    slopes = slopes[:, :docs] + slopes[:, docs : 2 * docs] + slopes[:, 2 * docs :]
    lane = lax.broadcasted_iota(jnp.int32, (1, docs), 1)
    lens = jnp.zeros((1, docs), jnp.int32)
    for j in range(docs):
        lens = jnp.where(lane == j, lens_ref[0, j], lens)
    slopes = (slopes / lens.astype(jnp.float32) * loss_scale).astype(jnp.bfloat16)
    slopes = [slopes[h * half : (h + 1) * half] for h in range(2 * heads)]
    seg, _ = document_of(lens_ref, docs, (1, seq_len), 1)
    member = lax.broadcasted_iota(jnp.int32, (docs, seq_len), 0) == seg
    me = lax.axis_index(HEAD)
    shares = []
    for owner in (me, me ^ 1):
        sums = got_ref[owner, :, features:]
        sums = jnp.concatenate([sums[:heads], sums[heads : 2 * heads]], axis=1)
        shares += [jnp.where(member, sums[h : h + 1], 0.0) for h in range(heads)]
    out = jnp.dot(
        jnp.concatenate(slopes * 3, axis=1),
        three_terms(jnp.concatenate(shares, axis=0)),
        preferred_element_type=jnp.float32,
    )
    out_ref[...] = out.astype(jnp.bfloat16)


def per_device(attn_queries, keys, values, out_weight, lengths, queries, positives):
    seq_len, width = attn_queries.shape
    heads = width // HD
    docs = lengths.shape[1]
    features = out_weight.shape[1]
    split = lax.axis_size(HEAD)
    cores = lax.axis_size(DP[3])
    others = lax.axis_size(DP[:3])
    lanes = 2 * others
    f32, bf16 = jnp.float32, jnp.bfloat16
    big = pltpu.CompilerParams(vmem_limit_bytes=60 * 2**20)
    small = pltpu.CompilerParams(vmem_limit_bytes=16 * 2**20)

    half = HD // 2
    line = (*DP[:3], *HEAD)
    groups = class_groups()

    partial, wanted = pl.pallas_call(
        attend_kernel,
        out_shape=(
            jax.ShapeDtypeStruct((split, docs, features + seq_len // 2), f32),
            jax.ShapeDtypeStruct((heads * half, features), bf16),
        ),
        in_specs=[SMEM] + [VMEM] * 5,
        out_specs=(VMEM, VMEM),
        scratch_shapes=[pltpu.VMEM((seq_len, HD), f32)],
        compiler_params=big,
        name="attend",
    )(lengths, attn_queries, keys, values, out_weight, queries)
    got = lax.all_to_all(partial, HEAD, 0, 0, tiled=True)
    their_rows = lax.ppermute(wanted, HEAD, [(i, i ^ 1) for i in range(split)])
    rows, whole = pl.pallas_call(
        copies_kernel,
        out_shape=(
            jax.ShapeDtypeStruct((others, 2, features // 2), bf16),
            jax.ShapeDtypeStruct((docs, features), f32),
        ),
        in_specs=[VMEM],
        out_specs=(VMEM, VMEM),
        compiler_params=small,
        name="copies",
    )(got)
    every = lax.all_to_all(rows, line, 0, 0, axis_index_groups=groups, tiled=True)
    every = every.reshape(lanes, features // 2)
    pos = positives.reshape(others, cores * split)
    whole, their_rows = lax.optimization_barrier((whole, their_rows))
    uppers = lax.axis_size(DP[2])
    across = [[i, i ^ (split + 2)] for i in range(split)]
    whole = lax.all_gather(whole, DP[3])
    unit, rnorm, rounded = pl.pallas_call(
        unit_kernel,
        out_shape=(
            jax.ShapeDtypeStruct((cores * docs, features), f32),
            jax.ShapeDtypeStruct((cores * docs, HD), f32),
            jax.ShapeDtypeStruct((cores * docs, features), bf16),
        ),
        in_specs=[VMEM],
        out_specs=(VMEM,) * 3,
        compiler_params=small,
        name="unit",
    )(whole)
    units = lax.all_gather(rounded, (DP[2], *HEAD), axis_index_groups=across)

    stats, logits, chosen = pl.pallas_call(
        logits_kernel,
        out_shape=(
            jax.ShapeDtypeStruct((others // uppers, 2, lanes), f32),
            jax.ShapeDtypeStruct((cores * docs, lanes), f32),
            jax.ShapeDtypeStruct((cores * docs, lanes), f32),
        ),
        in_specs=[VMEM] * 3,
        out_specs=(VMEM,) * 3,
        compiler_params=small,
        name="logits",
    )(units, every, pos)
    stats = lax.all_to_all(stats, DP[:2], 0, 0, tiled=True)

    grads = pl.pallas_call(
        slopes_kernel,
        out_shape=jax.ShapeDtypeStruct((cores * split, docs, features + lanes), bf16),
        in_specs=[VMEM] * 6,
        out_specs=VMEM,
        compiler_params=small,
        name="slopes",
    )(stats, logits, chosen, unit, rnorm, every)
    grads = lax.all_to_all(grads, (DP[3], *HEAD), 0, 0, tiled=True)

    d_values, loss = pl.pallas_call(
        values_kernel,
        out_shape=(
            jax.ShapeDtypeStruct((half, seq_len), bf16),
            jax.ShapeDtypeStruct((1, 1), f32),
        ),
        in_specs=[SMEM] + [VMEM] * 4,
        out_specs=(VMEM, VMEM),
        compiler_params=small,
        name="slopes_of_values",
    )(lengths, grads, out_weight, their_rows, got)
    return d_values.T, loss.reshape(())


def solution(mesh):
    shape = (4, 8, 2, 2) if mesh.devices.size == 512 else (1, mesh.devices.size // 16, 2, 2)
    head = mesh.shape["head"]
    torus = Mesh(mesh.devices.reshape(*shape, head // 2, 2), (*DP, *HEAD))
    placed = (
        P(DP, HEAD),
        P(DP, None),
        P(DP, None),
        P(HEAD, None),
        P(DP, None),
        P(DP, HEAD),
        P(),
    )
    return jax.shard_map(
        per_device, mesh=torus, in_specs=placed, out_specs=(P(DP, HEAD), P()), check_vma=False
    )
```

```python
import math

import jax
import jax.numpy as jnp
from jax import lax
from jax.experimental import pallas as pl
from jax.experimental.pallas import tpu as pltpu
from jax.sharding import Mesh
from jax.sharding import PartitionSpec as P

HEADS = 12
KV_HEADS = 2
HD = 128
DP = ("dp_0", "dp_1", "dp_2", "dp_3")
LONGEST = 256
HEAD = ("head_0", "head_1")

sim_scale = 20.0
loss_scale = 32768.0

NT = (((1,), (1,)), ((), ()))
TN = (((0,), (0,)), ((), ()))
VMEM = pl.BlockSpec(memory_space=pltpu.VMEM)
SMEM = pl.BlockSpec(memory_space=pltpu.SMEM)


def query_class():
    return lax.axis_index(HEAD) ^ (2 * lax.axis_index(DP[2]))


def class_groups():
    split, uppers = lax.axis_size(HEAD), lax.axis_size(DP[2])
    blocks = lax.axis_size(DP[:2])
    return [
        [(b * uppers + u) * split + (k ^ (2 * u)) for b in range(blocks) for u in range(uppers)]
        for k in range(split)
    ]


def three_terms(value):
    high = value.astype(jnp.bfloat16)
    rest = value - high.astype(jnp.float32)
    mid = rest.astype(jnp.bfloat16)
    low = (rest - mid.astype(jnp.float32)).astype(jnp.bfloat16)
    return jnp.concatenate([high, mid, low], axis=0)


def of_three(value):
    rows = value.shape[0] // 3
    return value[:rows] + value[rows : 2 * rows] + value[2 * rows :]


def exact_dot(value, other, dims):
    return of_three(
        lax.dot_general(three_terms(value), other, dims, preferred_element_type=jnp.float32)
    )


def document_of(lens_ref, docs, shape, dim):
    place = lax.broadcasted_iota(jnp.int32, shape, dim)
    seg = jnp.zeros(shape, jnp.int32)
    start = jnp.zeros(shape, jnp.int32)
    end = jnp.int32(0)
    for j in range(docs):
        end = end + lens_ref[0, j]
        past = place >= end
        seg = seg + past.astype(jnp.int32)
        start = jnp.where(past, end, start)
    return seg, start


def lens_column(lens_ref, docs):
    row = lax.broadcasted_iota(jnp.int32, (docs, 1), 0)
    column = jnp.zeros((docs, 1), jnp.int32)
    for j in range(docs):
        column = jnp.where(row == j, lens_ref[0, j], column)
    return column.astype(jnp.float32)


def attend_kernel(
    lens_ref, q_ref, k_ref, v_ref, w_ref, queries_ref, sent_ref, sums_ref, rows_ref, total
):
    seq_len, width = q_ref.shape
    heads = width // HD
    docs = lens_ref.shape[1]
    kv_head = lax.axis_index(HEAD) * heads // (HEADS // KV_HEADS)
    columns = pl.ds(pl.multiple_of(kv_head * HD, HD), HD)
    seg, start = document_of(lens_ref, docs, (1, seq_len), 1)
    total[...] = jnp.zeros_like(total)
    block = min(128, seq_len)
    factor = math.log2(math.e) / math.sqrt(HD)
    lane = lax.broadcasted_iota(jnp.int32, (block, HD), 1)
    for first in range(0, seq_len, block):
        low = max(0, (first - LONGEST + 1) // block * block)
        span = first + block - low
        k_block = k_ref[low : first + block, columns]
        k_place = low + lax.broadcasted_iota(jnp.int32, (span, block), 0)
        q_place = first + lax.broadcasted_iota(jnp.int32, (span, block), 1)
        allowed = (k_place <= q_place) & (k_place >= start[:, first : first + block])
        for h in range(heads):
            q_block = q_ref[first : first + block, h * HD : (h + 1) * HD]
            scores = lax.dot_general(k_block, q_block, NT, preferred_element_type=jnp.float32)
            scores = jnp.where(allowed, scores, -1e30)
            top = jnp.max(scores, axis=0, keepdims=True)
            expo = jnp.exp2((scores - top) * factor)
            norm = 1.0 / jnp.sum(expo, axis=0, keepdims=True)
            probs = (expo * norm).astype(jnp.bfloat16)
            pick = (lane == h).astype(jnp.bfloat16)
            total[low : first + block, :] += jnp.dot(
                probs, pick, preferred_element_type=jnp.float32
            )
    by_head = total[...].T
    member = lax.broadcasted_iota(jnp.int32, (docs, seq_len), 0) == seg
    shares = jnp.concatenate(
        [jnp.where(member, by_head[h : h + 1, :], 0.0) for h in range(heads)], axis=0
    )
    sums = exact_dot(shares, v_ref[:, columns], (((1,), (0,)), ((), ())))
    pooled = jnp.concatenate(
        [sums[h * docs : (h + 1) * docs] for h in range(heads)], axis=1
    ) / lens_column(lens_ref, docs)
    emb = exact_dot(pooled, w_ref[...], (((1,), (0,)), ((), ())))
    features = emb.shape[1]
    queries = queries_ref[...].astype(jnp.float32)
    place = lax.broadcasted_iota(jnp.int32, queries.shape, 0)
    rest = jnp.zeros((docs - heads, HD), jnp.float32)
    for k in range(sent_ref.shape[0]):
        row = jnp.where(place == k ^ (2 * lax.axis_index(DP[2])), queries, 0.0)
        row = jnp.sum(row, axis=0, keepdims=True)
        chunks = [row[:, c * HD : (c + 1) * HD] for c in range(heads)]
        sent_ref[k, :, :features] = emb
        sent_ref[k, :, features:] = jnp.concatenate([*chunks, rest], axis=0)
    sums_ref[...] = by_head[:docs]
    left = jnp.concatenate([by_head[h : h + 1] for h in range(heads)], axis=1)
    lines = []
    for _ in range(3):
        term = left.astype(jnp.bfloat16).astype(jnp.float32)
        lines.append(term)
        left = left - term
    lines.append(jnp.zeros((13, features), jnp.float32))
    rows_ref[heads * (HD // 2) :, :] = jnp.concatenate(lines, axis=0).astype(jnp.bfloat16)
    half = HD // 2
    for h in range(heads):
        place = pl.multiple_of(h * HD + (1 - lax.axis_index(HEAD[1])) * half, half)
        rows_ref[h * half : (h + 1) * half, :] = w_ref[pl.ds(place, half), :]


def copies_kernel(got_ref, out_ref, whole_ref):
    docs, features = whole_ref.shape
    split = got_ref.shape[0]
    width = features // split
    parts = []
    for k in range(split):
        line = got_ref[k, :, features:]
        parts += [line[c : c + 1] for c in range(width // HD)]
    middle = len(parts) // 2
    halves = [jnp.concatenate(parts[:middle], axis=1), jnp.concatenate(parts[middle:], axis=1)]
    both = jnp.concatenate(halves, axis=0).astype(jnp.bfloat16)
    out_ref[...] = jnp.broadcast_to(both[None], out_ref.shape)
    whole = got_ref[0, :, :features]
    for k in range(1, split):
        whole = whole + got_ref[k, :, :features]
    whole_ref[...] = whole


def pair_logits(unit, q_ref):
    half = q_ref.shape[1]
    docs = unit.shape[0]
    both = jnp.concatenate([unit[:, :half], unit[:, half:]], axis=0)
    parts = lax.dot_general(both, q_ref[...], NT, preferred_element_type=jnp.float32)
    even = lax.broadcasted_iota(jnp.int32, (docs, q_ref.shape[0]), 1) % 2 == 0
    mine = jnp.where(even, parts[:docs], parts[docs:])
    width = mine.shape[1]
    other = jnp.where(even, pltpu.roll(mine, width - 1, 1), pltpu.roll(mine, 1, 1))
    return sim_scale * (mine + other)


def positive_mask(pos_ref, docs):
    count, classes = pos_ref.shape
    mine = lax.broadcasted_iota(jnp.int32, (count, classes), 1) == (
        lax.axis_size(HEAD) * lax.axis_index(DP[3]) + query_class()
    )
    lane = lax.broadcasted_iota(jnp.int32, (count, 2 * count), 1)
    row = lax.broadcasted_iota(jnp.int32, (count, 2 * count), 0)
    spread = (lane // 2 == row).astype(jnp.bfloat16)
    pos = jnp.where(mine, pos_ref[...], 0)

    def spread_out(digit):
        lines = lax.dot_general(
            digit.astype(jnp.float32).astype(jnp.bfloat16), spread, TN,
            preferred_element_type=jnp.float32,
        )
        return jnp.sum(lines, axis=0, keepdims=True)

    positive = 128.0 * spread_out(pos // 128) + spread_out(pos % 128)
    me = lax.axis_index(DP[:3])
    row = lax.broadcasted_iota(jnp.int32, (docs, 2 * count), 0)
    owned = jnp.concatenate([me * docs + row, (me ^ 1) * docs + row], axis=0)
    return (positive == owned.astype(jnp.float32)).astype(jnp.float32)


def unit_kernel(emb_ref, unit_ref, rnorm_ref, rounded_ref):
    emb = jnp.concatenate([emb_ref[core] for core in range(emb_ref.shape[0])], axis=0)
    rnorm = 1.0 / jnp.sqrt(jnp.sum(emb * emb, axis=1, keepdims=True) + 1e-06)
    unit = emb * rnorm
    unit_ref[...] = unit
    rnorm_ref[...] = jnp.broadcast_to(rnorm, rnorm_ref.shape)
    rounded_ref[...] = unit.astype(jnp.bfloat16)


def logits_kernel(units_ref, q_ref, pos_ref, out_ref, logits_ref, chosen_ref):
    docs = logits_ref.shape[0]
    me = lax.axis_index(DP[2])
    logits = pair_logits(jnp.concatenate([units_ref[me], units_ref[1 - me]], axis=0), q_ref)
    chosen = positive_mask(pos_ref, docs)
    top = jnp.max(logits, axis=0, keepdims=True)
    expo = jnp.exp(logits - top)
    total = jnp.sum(expo[:docs], axis=0, keepdims=True) + jnp.sum(expo[docs:], axis=0, keepdims=True)
    lse = top + jnp.log(total)
    hits = logits * chosen
    positive = jnp.sum(hits[:docs], axis=0, keepdims=True) + jnp.sum(
        hits[docs:], axis=0, keepdims=True
    )
    out_ref[...] = jnp.broadcast_to(
        jnp.concatenate([lse, positive], axis=0)[None], out_ref.shape
    )
    logits_ref[...] = logits[:docs]
    chosen_ref[...] = chosen[:docs]


def slopes_kernel(stats_ref, logits_ref, chosen_ref, unit_ref, rnorm_ref, q_ref, out_ref):
    pair_docs = logits_ref.shape[0]
    half = q_ref.shape[1]
    features = 2 * half
    split = out_ref.shape[0] // 2
    docs = pair_docs // 2
    each = stats_ref[:, 0, :]
    top = jnp.max(each, axis=0, keepdims=True)
    lse = top + jnp.log(jnp.sum(jnp.exp(each - top), axis=0, keepdims=True))
    positive = jnp.sum(stats_ref[:, 1, :], axis=0, keepdims=True)
    slopes = jnp.exp(logits_ref[...] - lse) - chosen_ref[...]
    even = lax.broadcasted_iota(jnp.int32, slopes.shape, 1) % 2 == 0
    both = jnp.concatenate([jnp.where(even, slopes, 0.0), jnp.where(even, 0.0, slopes)], axis=0)
    parts = sim_scale * exact_dot(both, q_ref[...], (((1,), (0,)), ((), ())))
    grads = jnp.concatenate([parts[:pair_docs], parts[pair_docs:]], axis=1)
    unit = unit_ref[...]
    inner = jnp.sum(unit * grads, axis=1, keepdims=True)
    grads = (rnorm_ref[:, :1] * (grads - unit * inner)).astype(jnp.bfloat16)
    losses = jnp.broadcast_to(lse - positive, (docs, lse.shape[1]))
    row = lax.broadcasted_iota(jnp.int32, losses.shape, 0)
    high = losses.astype(jnp.bfloat16).astype(jnp.float32)
    mid = (losses - high).astype(jnp.bfloat16).astype(jnp.float32)
    losses = jnp.where(row == 0, high, jnp.where(row == 1, mid, losses - high - mid))
    for k in range(2 * split):
        core = k // split
        out_ref[k, :, :features] = grads[core * docs : (core + 1) * docs]
        out_ref[k, :, features:] = losses.astype(jnp.bfloat16)


def values_kernel(lens_ref, grads_ref, my_rows_ref, their_rows_ref, sums_ref, out_ref, loss_ref):
    docs = lens_ref.shape[1]
    features = my_rows_ref.shape[1]
    seq_len = out_ref.shape[1]
    half = HD // 2
    heads = my_rows_ref.shape[0] // HD
    low = lax.axis_index(HEAD[1])
    grads = grads_ref[0].astype(jnp.float32)
    for k in range(1, grads_ref.shape[0]):
        grads = grads + grads_ref[k].astype(jnp.float32)
    lanes = grads.shape[1] - features
    loss_ref[...] = jnp.sum(
        jnp.sum(grads[:3, features:], axis=0, keepdims=True), axis=1, keepdims=True
    ) / (grads_ref.shape[0] * lanes)
    terms = three_terms(grads[:, :features])
    lens = lens_column(lens_ref, docs)
    slopes = []
    for h in range(heads):
        rows = my_rows_ref[pl.ds(pl.multiple_of(h * HD + low * half, half), half), :]
        slopes.append(lax.dot_general(terms, rows, NT, preferred_element_type=jnp.float32))
    for h in range(heads):
        rows = their_rows_ref[h * half : (h + 1) * half, :]
        slopes.append(lax.dot_general(terms, rows, NT, preferred_element_type=jnp.float32))
    slopes = [(of_three(part) / lens * loss_scale).astype(jnp.bfloat16) for part in slopes]
    seg, _ = document_of(lens_ref, docs, (1, seq_len), 1)
    member = lax.broadcasted_iota(jnp.int32, (docs, seq_len), 0) == seg
    mine = [jnp.where(member, sums_ref[h : h + 1], 0.0) for h in range(heads)]
    lines = their_rows_ref[heads * half :, :].astype(jnp.float32)
    theirs = [
        jnp.where(member, lines[t : t + 1, h * seq_len : (h + 1) * seq_len], 0.0)
        for t in range(3)
        for h in range(heads)
    ]
    shares = jnp.concatenate(
        [
            three_terms(jnp.concatenate(mine, axis=0)),
            jnp.concatenate(theirs, axis=0).astype(jnp.bfloat16),
        ],
        axis=0,
    )
    out = lax.dot_general(
        jnp.concatenate(slopes[:heads] * 3 + slopes[heads:] * 3, axis=0),
        shares,
        TN,
        preferred_element_type=jnp.float32,
    )
    out_ref[...] = out.astype(jnp.bfloat16)


def per_device(attn_queries, keys, values, out_weight, lengths, queries, positives):
    seq_len, width = attn_queries.shape
    heads = width // HD
    docs = lengths.shape[1]
    features = out_weight.shape[1]
    split = lax.axis_size(HEAD)
    cores = lax.axis_size(DP[3])
    others = lax.axis_size(DP[:3])
    lanes = 2 * others
    f32, bf16 = jnp.float32, jnp.bfloat16
    big = pltpu.CompilerParams(vmem_limit_bytes=60 * 2**20)
    small = pltpu.CompilerParams(vmem_limit_bytes=16 * 2**20)

    half = HD // 2
    line = (*DP[:3], *HEAD)
    groups = class_groups()

    partial, sums, wanted = pl.pallas_call(
        attend_kernel,
        out_shape=(
            jax.ShapeDtypeStruct((split, docs, features + HD), f32),
            jax.ShapeDtypeStruct((docs, seq_len), f32),
            jax.ShapeDtypeStruct((heads * half + 16, features), bf16),
        ),
        in_specs=[SMEM] + [VMEM] * 5,
        out_specs=(VMEM,) * 3,
        scratch_shapes=[pltpu.VMEM((seq_len, HD), f32)],
        compiler_params=big,
        name="attend",
    )(lengths, attn_queries, keys, values, out_weight, queries)
    got = lax.all_to_all(partial, HEAD, 0, 0, tiled=True)
    their_rows = lax.ppermute(wanted, HEAD, [(i, i ^ 1) for i in range(split)])
    rows, whole = pl.pallas_call(
        copies_kernel,
        out_shape=(
            jax.ShapeDtypeStruct((others, 2, features // 2), bf16),
            jax.ShapeDtypeStruct((docs, features), f32),
        ),
        in_specs=[VMEM],
        out_specs=(VMEM, VMEM),
        compiler_params=small,
        name="copies",
    )(got)
    every = lax.all_to_all(rows, line, 0, 0, axis_index_groups=groups, tiled=True)
    every = every.reshape(lanes, features // 2)
    pos = positives.reshape(others, cores * split)
    whole, their_rows = lax.optimization_barrier((whole, their_rows))
    uppers = lax.axis_size(DP[2])
    across = [[i, i ^ (split + 2)] for i in range(split)]
    whole = lax.all_gather(whole, DP[3])
    unit, rnorm, rounded = pl.pallas_call(
        unit_kernel,
        out_shape=(
            jax.ShapeDtypeStruct((cores * docs, features), f32),
            jax.ShapeDtypeStruct((cores * docs, HD), f32),
            jax.ShapeDtypeStruct((cores * docs, features), bf16),
        ),
        in_specs=[VMEM],
        out_specs=(VMEM,) * 3,
        compiler_params=small,
        name="unit",
    )(whole)
    units = lax.all_gather(rounded, (DP[2], *HEAD), axis_index_groups=across)

    stats, logits, chosen = pl.pallas_call(
        logits_kernel,
        out_shape=(
            jax.ShapeDtypeStruct((others // uppers, 2, lanes), f32),
            jax.ShapeDtypeStruct((cores * docs, lanes), f32),
            jax.ShapeDtypeStruct((cores * docs, lanes), f32),
        ),
        in_specs=[VMEM] * 3,
        out_specs=(VMEM,) * 3,
        compiler_params=small,
        name="logits",
    )(units, every, pos)
    stats = lax.all_to_all(stats, DP[:2], 0, 0, tiled=True)

    grads = pl.pallas_call(
        slopes_kernel,
        out_shape=jax.ShapeDtypeStruct((cores * split, docs, features + lanes), bf16),
        in_specs=[VMEM] * 6,
        out_specs=VMEM,
        compiler_params=small,
        name="slopes",
    )(stats, logits, chosen, unit, rnorm, every)
    grads = lax.all_to_all(grads, (DP[3], *HEAD), 0, 0, tiled=True)

    d_values, loss = pl.pallas_call(
        values_kernel,
        out_shape=(
            jax.ShapeDtypeStruct((half, seq_len), bf16),
            jax.ShapeDtypeStruct((1, 1), f32),
        ),
        in_specs=[SMEM] + [VMEM] * 4,
        out_specs=(VMEM, VMEM),
        compiler_params=small,
        name="slopes_of_values",
    )(lengths, grads, out_weight, their_rows, sums)
    return d_values.T, loss.reshape(())


def solution(mesh):
    shape = (4, 8, 2, 2) if mesh.devices.size == 512 else (1, mesh.devices.size // 16, 2, 2)
    head = mesh.shape["head"]
    torus = Mesh(mesh.devices.reshape(*shape, head // 2, 2), (*DP, *HEAD))
    placed = (
        P(DP, HEAD),
        P(DP, None),
        P(DP, None),
        P(HEAD, None),
        P(DP, None),
        P(DP, HEAD),
        P(),
    )
    return jax.shard_map(
        per_device, mesh=torus, in_specs=placed, out_specs=(P(DP, HEAD), P()), check_vma=False
    )
```
